256 devices in a mesh: group: 4 (over z_lo, core), fsdp: 64 (over y, z_hi, x).
Axes of the slice: x: 4, y: 4, z: 8 (z_hi: 4, z_lo: 2; z = z_hi * 2 + z_lo), core: 2. Of those that a mesh axis runs over, the one named last changes fastest.
Arguments:
- head_out: bfloat16 [4, 24576, 2048], P('group', 'fsdp'), may hold values from -6 to 6
- gate_in: bfloat16 [4, 24576, 2048], P('group', 'fsdp'), may hold values from -8 to 8
- cotangent: bfloat16 [4, 24576, 2048], P('group', 'fsdp'), may hold values from -6 to 6
- momentum: float32 [4, 2048, 2048], P('group', 'fsdp'), may hold values from -6 to 6
- chosen_index: int32 [4, 2048, 512], P('group', 'fsdp'), may hold values from 0 to 63, as said below
- out_weight: bfloat16 [2048, 2048], P('fsdp'), may hold values from -0.125 to 0.125
- norm_gain: float32 [128], replicated, may hold values from 0.1 to 1.9
Outputs:
- head_grad: bfloat16 [4, 24576, 2048], P('group', 'fsdp')
- gate_grad: bfloat16 [4, 24576, 2048], P('group', 'fsdp')
- new_momentum: float32 [4, 2048, 2048], P('group', 'fsdp')
- update: float32 [2048, 2048], P('fsdp')
The draws below stay inside these ranges and needn't reach their ends.
Inputs may be any that keep to these rules, and one draw needn't show every extreme that they name: `chosen_index`: within each transform block, the 16 entries of a group are distinct.
All inputs are finite; a program needn't handle non-finite values.
Results may differ from the reference program's by a relative error of at most 0.0022.
Values may be sent and summed in bfloat16 or wider, within the bound.
A program may use at most 128 MiB of HBM per device.

```python
import jax
import jax.numpy as jnp
from jax import lax

HDIM = 128
M = 2048
SPAN = 64
KEEP = 16
GROUPS = 4
TOKENS = 24576
HK = 2048
BLOCKS = 32


def draw_chosen_index(key, part):
    key = jax.random.fold_in(key, 7)
    scores = jax.random.randint(key, (GROUPS, HK, BLOCKS, SPAN), 0, 2 ** 20) * SPAN
    scores = scores + jnp.arange(SPAN, dtype=jnp.int32)
    chosen = lax.top_k(scores, KEEP)[1]
    return chosen.reshape(GROUPS, HK, BLOCKS * KEEP).astype(jnp.int32)


def block_scale(own_key, dims, split, low, high):
    def one(position, parts):
        steps = jax.random.uniform(jax.random.fold_in(jax.random.fold_in(own_key, 6), position), (parts,), jnp.float32, low / len(split), high / len(split))
        return jnp.repeat(jnp.exp(steps), dims[position] // parts).reshape((-1,) + (1,) * (len(dims) - position - 1))

    factor_of = one(*split[0])
    for cut in split[1:]:
        factor_of = factor_of * one(*cut)
    return factor_of


def centred(key, dims, scale, reach, cuts=(), kind=jnp.bfloat16):
    drawn = scale * jax.random.normal(key, dims, jnp.float32)
    if cuts:
        drawn = drawn * block_scale(key, dims, cuts, -0.22, 0.18)
    return jnp.clip(drawn, -reach, reach).astype(kind)


def setup_inputs(seed: int = 0) -> dict:
    splits = jax.random.split(jax.random.key(seed), 8)
    head_out = centred(splits[0], (GROUPS, TOKENS, HK), 1.0, 6.0, ((0, 4), (1, 64)))
    gate_in = centred(splits[1], (GROUPS, TOKENS, HK), 1.5, 8.0, ((0, 4), (1, 64)))
    cotangent = centred(splits[2], (GROUPS, TOKENS, M), 1.0, 6.0, ((0, 4), (1, 64)))
    momentum = centred(splits[3], (GROUPS, HK, M), 1.0, 6.0, ((0, 4), (1, 64)), jnp.float32)
    chosen_index = draw_chosen_index(jax.random.fold_in(splits[7], 71), 0)
    out_weight = centred(splits[5], (HK, M), M ** -0.5, 0.125, ((0, 64),))
    norm_gain = jnp.clip(1.0 + 0.18 * jax.random.normal(splits[6], (HDIM,), jnp.float32), 0.1, 1.9)
    return dict(head_out=head_out, gate_in=gate_in, cotangent=cotangent, momentum=momentum, chosen_index=chosen_index, out_weight=out_weight, norm_gain=norm_gain)


epsilon = 1e-06
decay_rate = 0.999

def cosine_table(width):
    freq = jnp.arange(width, dtype=jnp.float32)[:, None]
    place = jnp.arange(width, dtype=jnp.float32)[None, :]
    scale = jnp.where(freq == 0, jnp.sqrt(1.0 / width), jnp.sqrt(2.0 / width))
    return jnp.cos(jnp.pi * (place + 0.5) * freq / width) * scale

def gated_output(heads, gates, norm_gain):
    row_total = heads.shape[0]
    per_head = heads.reshape(row_total, -1, norm_gain.shape[0])
    scaled = per_head * lax.rsqrt(lax.optimization_barrier(jnp.mean(per_head * per_head, axis=-1, keepdims=True)) + epsilon)
    normed = (scaled * norm_gain).reshape(row_total, -1)
    return normed * jax.nn.silu(gates)

def pick_table(where):
    return (where[..., None] == jnp.arange(SPAN, dtype=jnp.int32)).astype(jnp.float32)

def reference(head_out, gate_in, cotangent, momentum, chosen_index, out_weight, norm_gain):
    highest = lax.Precision.HIGHEST
    cosine = cosine_table(SPAN)
    head_list, gate_list, moment_list = ([], [], [])
    total = jnp.zeros((HK, BLOCKS, SPAN), jnp.float32)
    for member in range(GROUPS):
        heads = head_out[member].astype(jnp.float32)
        gates = gate_in[member].astype(jnp.float32)
        upstream_in = cotangent[member]
        gated, pullback = jax.vjp(lambda a, b: gated_output(a, b, norm_gain), heads, gates)
        gated_low = gated.astype(jnp.bfloat16)
        gradient = jnp.dot(gated_low.T, upstream_in, preferred_element_type=jnp.float32) * TOKENS ** (-0.5)
        upstream = jnp.dot(upstream_in, out_weight.T, preferred_element_type=jnp.float32)
        head_grad, gate_grad = pullback(upstream)
        head_list.append(head_grad.astype(jnp.bfloat16))
        gate_list.append(gate_grad.astype(jnp.bfloat16))
        moment = decay_rate * momentum[member] + gradient
        blocked = moment.reshape(HK, BLOCKS, SPAN)
        coeffs = jnp.einsum('rck,fk->rcf', blocked, cosine, precision=highest)
        onehot = pick_table(chosen_index[member].reshape(HK, BLOCKS, KEEP))
        kept = jnp.einsum('rcf,rcjf->rcj', coeffs, onehot, precision=highest)
        own = jnp.einsum('rcj,rcjf->rcf', kept, onehot, precision=highest)
        moment_list.append(moment - jnp.einsum('rcf,fk->rck', own, cosine, precision=highest).reshape(HK, M))
        total = total + own
    update = (jnp.einsum('rcf,fk->rck', total, cosine, precision=highest) / GROUPS).reshape(HK, M)
    return (jnp.stack(head_list), jnp.stack(gate_list), jnp.stack(moment_list), update)
```

```python
import functools

import jax
import jax.numpy as jnp
import numpy as np
from jax import lax
from jax.experimental import pallas as pl
from jax.experimental.pallas import tpu as pltpu
from jax.sharding import PartitionSpec as P

MESH = pl.DeviceIdType.MESH
HIGHEST = lax.Precision.HIGHEST
F32 = jnp.float32
BF16 = jnp.bfloat16

SPAN = 64
KEEP = 16
HDIM = 128
TOK = 384
WIDTH = 2048
ROWS = 32
SUB = 512
EPS = 1e-06
DECAY = 0.999

PIECES = ((0, 0), (1, 0), (0, 1), (1, 1))
DOWN_ORDER = (0, 2, 3, 1)


def remote(src, dst, send, recv, device):
    return pltpu.make_async_remote_copy(
        src_ref=src, dst_ref=dst, send_sem=send, recv_sem=recv, device_id=device, device_id_type=MESH
    )


def kernel(
    head_hbm, gate_hbm, cot_hbm, mom_hbm, idx_hbm, w_hbm, gain_ref, dct_ref, idct_ref,
    hgrad_hbm, ggrad_hbm, newmom_hbm, update_hbm,
    heads, gates, cot, mom, idx, w6, low, gsend, gt, cslot, p2s, p2r, q, p3r, dec, dec_r, pair, pair_r,
    newmom, update, perm, spread, upb, hgrad, ggrad,
    load_sem, own_sem, out_sem,
    wx_s, wx_r, wy_s, wy_r, up_s, up_r, dn_s, dn_r, sib_s, sib_r,
    c1_s, c1_r, c2_s, c2_r, gt_s, gt_r, s2_s, s2_r, s3_s, s3_r, d_s, d_r, e_s, e_r,
):
    f = lax.axis_index("fsdp")
    g = lax.axis_index("group")
    y, z, x = f // 16, (f // 4) % 4, f % 4
    lo, core = g // 2, g % 2
    sibling = {"fsdp": f, "group": g + 1 - 2 * core}
    across = {"fsdp": f, "group": (g + 2) % 4}
    above = {"fsdp": y * 16 + ((z + lo) % 4) * 4 + x, "group": (g + 2) % 4}
    below = {"fsdp": y * 16 + ((z + 3 + lo) % 4) * 4 + x, "group": (g + 2) % 4}

    def at_x(d):
        return {"fsdp": y * 16 + z * 4 + (x + d) % 4, "group": g}

    def at_y(d):
        return {"fsdp": ((y + d) % 4) * 16 + z * 4 + x, "group": g}

    def at_z(d):
        return {"fsdp": y * 16 + ((z + d) % 4) * 4 + x, "group": g}

    along = (at_x, at_y)
    mine = (x, y)

    barrier = pltpu.get_barrier_semaphore()
    partners = [at(d) for at in (at_x, at_y, at_z) for d in (1, 2, 3)] + [sibling, above, below]
    for device in partners:
        pl.semaphore_signal(barrier, inc=1, device_id=device, device_id_type=MESH)
    pl.semaphore_wait(barrier, len(partners))

    def wx(d):
        half = w_hbm.at[pl.ds(pl.multiple_of(core * 16, 16), 16)]
        return remote(half, w6.at[y, z, x, core], wx_s.at[d - 1], wx_r.at[d - 1], at_x(d))

    def wy(d):
        part = w6.at[y, z, :, core]
        return remote(part, part, wy_s.at[d - 1], wy_r.at[d - 1], at_y(d))

    def up(p):
        part = w6.at[(y + p % 4) % 4, (z + 8 - p // 4 - 1 + lo) % 4, :, core]
        return remote(part, part, up_s.at[p], up_r.at[p], above)

    def down_piece(p):
        return DOWN_ORDER[p] if p < 4 else p - 2

    def down(p):
        part = w6.at[(y + down_piece(p)) % 4, (z + p // 4 + lo) % 4, :, core]
        return remote(part, part, dn_s.at[p], dn_r.at[p], below)

    def to_sibling(n):
        if n < 4:
            part = w6.at[(y + n) % 4, z, :, core]
        elif n < 10:
            part = w6.at[(y + (n - 4) % 4) % 4, (z + 3 - (n - 4) // 4) % 4, :, core]
        else:
            part = w6.at[(y + down_piece(n - 10)) % 4, (z + 1 + (n - 10) // 4) % 4, :, core]
        return remote(part, part, sib_s.at[n], sib_r.at[n], sibling)

    def first(axis, s, way):
        src = cot_hbm.at[:, pl.ds((axis * 2 + s) * SUB, SUB)]
        dst = cslot.at[axis, s, mine[axis]]
        return remote(src, dst, c1_s.at[axis, s, way], c1_r.at[axis, s, way], along[axis](1 + 2 * way))

    def second(axis, s, way):
        part = cslot.at[axis, s, (mine[axis] + 3 + 2 * way) % 4, pl.ds(way * (TOK // 2), TOK // 2)]
        return remote(part, part, c2_s.at[axis, s, way], c2_r.at[axis, s, way], along[axis](1 + 2 * way))

    def gated_to(axis, d):
        src = gsend.at[axis, (mine[axis] + d) % 4]
        dst = gt.at[axis, :, pl.ds(pl.multiple_of(mine[axis] * TOK, 128), TOK)]
        return remote(src, dst, gt_s.at[axis, d - 1], gt_r.at[axis, d - 1], along[axis](d))

    def own_gated(axis):
        src = gsend.at[axis, mine[axis]]
        dst = gt.at[axis, :, pl.ds(pl.multiple_of(mine[axis] * TOK, 128), TOK)]
        return pltpu.make_async_copy(src, dst, own_sem.at[axis])

    def stage2(n, d):
        return remote(
            p2s.at[n, d - 1], p2r.at[n, d - 1], s2_s.at[n, d - 1], s2_r.at[n, d - 1], along[1 - PIECES[n][0]](d)
        )

    def stage3(n, d):
        src = q.at[n, pl.ds(pl.multiple_of(((z + d) % 4) * ROWS, ROWS), ROWS)]
        return remote(src, p3r.at[n, d - 1], s3_s.at[n, d - 1], s3_r.at[n, d - 1], at_z(d))

    def to_pair(n):
        return remote(dec.at[n], dec_r.at[n], d_s.at[n], d_r.at[n], sibling)

    def to_across(n):
        return remote(pair.at[n], pair_r.at[n], e_s.at[n], e_r.at[n], across)

    loads = [
        pltpu.make_async_copy(head_hbm, heads, load_sem.at[0]),
        pltpu.make_async_copy(gate_hbm, gates, load_sem.at[1]),
        pltpu.make_async_copy(
            w_hbm.at[pl.ds(pl.multiple_of(core * 16, 16), 16)], w6.at[y, z, x, core], load_sem.at[2]
        ),
    ]
    for axis in range(2):
        for s in range(2):
            loads.append(
                pltpu.make_async_copy(
                    cot_hbm.at[:, pl.ds((axis * 2 + s) * SUB, SUB)],
                    cslot.at[axis, s, mine[axis]],
                    load_sem.at[3 + axis * 2 + s],
                )
            )
    loads += [
        pltpu.make_async_copy(cot_hbm, cot, load_sem.at[7]),
        pltpu.make_async_copy(mom_hbm, mom, load_sem.at[8]),
        pltpu.make_async_copy(idx_hbm, idx, load_sem.at[9]),
    ]
    for d in (1, 2, 3):
        wx(d).start()
    for load in loads[:3]:
        load.start()
    for axis in range(2):
        for way in range(2):
            first(axis, 0, way).start()
    for load in loads[3:]:
        load.start()

    row = lax.broadcasted_iota(jnp.int32, (SUB, SUB), 0)
    col = lax.broadcasted_iota(jnp.int32, (SUB, SUB), 1)
    source = ((row >> 5) & 3) * 128 + (row >> 7) * 32 + (row & 31)
    perm[0] = jnp.where(source == col, 1.0, 0.0).astype(BF16)
    perm[1] = jnp.where(row == col, 1.0, 0.0).astype(BF16)
    quarter, block = row >> 7, (row >> 4) & 7
    spread[...] = jnp.where((block == (col >> 6)) & (quarter == ((col >> 4) & 3)), 1.0, 0.0).astype(BF16)

    gain = gain_ref[...]
    loads[0].wait()
    loads[1].wait()

    def gated_rows(i, carry):
        rows = pl.ds(pl.multiple_of(i * 32, 32), 32)
        for k in range(WIDTH // HDIM):
            cols = slice(k * HDIM, (k + 1) * HDIM)
            h = heads[rows, cols].astype(F32)
            a = gates[rows, cols].astype(F32)
            n = h * lax.rsqrt(jnp.mean(h * h, axis=-1, keepdims=True) + EPS)
            low[rows, cols] = ((n * gain) * (a * jax.nn.sigmoid(a))).astype(BF16)
        return carry

    lax.fori_loop(0, 6, gated_rows, 0)

    loads[2].wait()
    for d in (1, 2, 3):
        wx(d).wait_recv()
    for d in (1, 2, 3):
        wy(d).start()

    @pl.when(lo == 1)
    def _():
        up(0).start()

    @pl.when(lo == 0)
    def _():
        down(0).start()

    to_sibling(0).start()

    lax.fori_loop(6, 12, gated_rows, 0)

    for axis in range(2):

        def turn(b, carry, axis=axis):
            part = low[:, pl.ds(pl.multiple_of(b * SUB, SUB), SUB)]
            out = lax.dot_general(
                perm[axis], part, (((1,), (1,)), ((), ())), preferred_element_type=F32
            ).astype(BF16)
            if axis == 0:
                for to in range(4):
                    gsend[0, to, pl.ds(pl.multiple_of(b * 128, 128), 128), :] = out[to * 128 : (to + 1) * 128]
            else:
                gsend[1, b] = out
            return carry

        lax.fori_loop(0, 4, turn, 0)
        for d in (2, 1, 3):
            gated_to(axis, d).start()
        own_gated(axis).start()

    for axis in range(2):
        for way in range(2):
            first(axis, 0, way).wait_recv()
        for way in range(2):
            second(axis, 0, way).start()
    for axis in range(2):
        for way in range(2):
            first(axis, 1, way).start()

    for d in (1, 2, 3):
        wy(d).wait_recv()

    @pl.when(lo == 1)
    def _():
        for p in (1, 2, 3):
            up(p).start()

    @pl.when(lo == 0)
    def _():
        for p in (1, 2, 3):
            down(p).start()

    for n in (1, 2, 3):
        to_sibling(n).start()

    def pass_on(p):
        up(p).wait_recv()

        @pl.when(lo == 0)
        def _():
            up(p).start()

        if p < 2:

            @pl.when(lo == 1)
            def _():
                up(p + 4).start()

        to_sibling(4 + p).start()
        down(p).wait_recv()

        @pl.when(lo == 1)
        def _():
            down(p).start()

        if p in (1, 2):

            @pl.when(lo == 0)
            def _():
                down(p + 3).start()

        to_sibling(10 + p).start()

    pass_on(0)

    def terms(n):
        axis, s = PIECES[n]
        right = cslot.at[axis, s]
        for d in (2, 1, 3, 0):
            owner = (mine[1 - axis] + d) % 4
            if axis == 0:
                left = gt[0, pl.ds(pl.multiple_of(owner * 128, 128), 128), :]
            else:
                left = jnp.concatenate(
                    [gt[1, pl.ds(pl.multiple_of(k * 128 + owner * 32, 32), 32), :] for k in range(4)], axis=0
                )
            part = jnp.dot(left, right[...].reshape(4 * TOK, SUB), preferred_element_type=F32)
            if d:
                p2s[n, d - 1] = part.astype(BF16)
                stage2(n, d).start()
            else:
                q[n] = part

    def pass_second(axis, s):
        for way in range(2):
            first(axis, s, way).wait_recv()
        for way in range(2):
            second(axis, s, way).start()

    def second_in(axis, s):
        for way in range(2):
            second(axis, s, way).wait_recv()

    def sum2(n):
        for d in (1, 2, 3):
            stage2(n, d).wait_recv()
        q[n] += (p2r[n, 0].astype(F32) + p2r[n, 1].astype(F32)) + p2r[n, 2].astype(F32)
        for d in (2, 1, 3):
            stage3(n, d).start()

    def gated_in(axis):
        own_gated(axis).wait()
        for d in (1, 2, 3):
            gated_to(axis, d).wait_recv()

    def moment_step(n):
        axis, s = PIECES[n]
        start = (axis * 2 + s) * SUB
        for d in (1, 2, 3):
            stage3(n, d).wait_recv()
        own = q[n, pl.ds(pl.multiple_of(z * ROWS, ROWS), ROWS), :]
        gradient = (own + p3r[n, 0]) + (p3r[n, 1] + p3r[n, 2])
        moment = DECAY * mom[:, start : start + SUB] + gradient * ((TOK * 64) ** -0.5)
        where = idx[:, start // 4 : start // 4 + 128]
        bits = jnp.left_shift(jnp.ones_like(where), where & 15)
        bits = jnp.concatenate(
            [jnp.where((where >> 4) == k, bits, 0).astype(F32).astype(BF16) for k in range(4)], axis=1
        )
        words = jnp.dot(bits, spread[...], preferred_element_type=F32).astype(jnp.int32)
        lane = lax.broadcasted_iota(jnp.int32, (ROWS, SUB), 1)
        chosen = (lax.shift_right_logical(words, lane & 15) & 1).astype(F32)

        def stacked(v):
            return jnp.concatenate([v[:, k * 128 : (k + 1) * 128] for k in range(4)], axis=0)

        coeffs = jnp.dot(stacked(moment), dct_ref[...], precision=HIGHEST, preferred_element_type=F32)
        decoded = jnp.dot(
            coeffs * stacked(chosen), idct_ref[...], precision=HIGHEST, preferred_element_type=F32
        )
        decoded = jnp.concatenate([decoded[k * ROWS : (k + 1) * ROWS] for k in range(4)], axis=1)
        dec[n] = decoded
        to_pair(n).start()
        newmom[n] = moment - decoded
        pltpu.make_async_copy(newmom.at[n], newmom_hbm.at[:, pl.ds(start, SUB)], out_sem.at[0, n]).start()

    def pair_step(n):
        to_pair(n).wait_recv()
        pair[n] = dec[n] + dec_r[n]
        to_across(n).start()

    def update_step(n):
        axis, s = PIECES[n]
        to_across(n).wait_recv()
        update[n] = (pair[n] + pair_r[n]) * 0.25
        start = (axis * 2 + s) * SUB
        pltpu.make_async_copy(update.at[n], update_hbm.at[:, pl.ds(start, SUB)], out_sem.at[1, n]).start()

    for load in loads[3:]:
        load.wait()
    for axis in range(2):
        gated_in(axis)
        second_in(axis, 0)
        terms(axis)
        pass_second(axis, 1)
        pass_on(1 + axis)
    sum2(0)
    sum2(1)
    pass_on(3)
    for axis in range(2):
        second_in(axis, 1)
        terms(2 + axis)
    pass_on(4)
    moment_step(0)
    moment_step(1)
    pass_on(5)
    sum2(2)
    sum2(3)
    pair_step(0)
    pair_step(1)

    for n in range(16):
        to_sibling(n).wait_recv()

    def grads_out(k, which):
        cols = pl.ds(pl.multiple_of(k * 256, 256), 256)
        src, dst = ((hgrad, hgrad_hbm), (ggrad, ggrad_hbm))[which]
        return pltpu.make_async_copy(src.at[k], dst.at[:, cols], out_sem.at[2 + which, k])

    def back(k, carry):
        weight = w6[k // 2, pl.ds((k % 2) * 2, 2)].reshape(256, WIDTH)
        upb[...] = lax.dot_general(
            cot[...], weight, (((1,), (1,)), ((), ())), preferred_element_type=F32
        )

        def back_rows(i, c):
            rows = pl.ds(pl.multiple_of(i * 32, 32), 32)
            for part in range(2):
                cols = pl.ds(pl.multiple_of(k * 256 + part * 128, 128), 128)
                here = slice(part * 128, (part + 1) * 128)
                h = heads[rows, cols].astype(F32)
                a = gates[rows, cols].astype(F32)
                u = upb[rows, here]
                r = lax.rsqrt(jnp.mean(h * h, axis=-1, keepdims=True) + EPS)
                n = h * r
                sig = jax.nn.sigmoid(a)
                ggrad[k, rows, here] = ((u * (n * gain)) * (sig * (1.0 + a * (1.0 - sig)))).astype(BF16)
                ds = (u * (a * sig)) * gain
                hgrad[k, rows, here] = (r * (ds - n * jnp.mean(ds * n, axis=-1, keepdims=True))).astype(BF16)
            return c

        lax.fori_loop(0, TOK // 32, back_rows, 0)
        grads_out(k, 0).start()
        grads_out(k, 1).start()
        return carry

    lax.fori_loop(0, 8, back, 0)

    for n in (2, 3):
        moment_step(n)
    update_step(0)
    update_step(1)
    for n in (2, 3):
        pair_step(n)
    for n in (2, 3):
        update_step(n)

    for d in (1, 2, 3):
        wx(d).wait_send()
        wy(d).wait_send()
        for axis in range(2):
            gated_to(axis, d).wait_send()
        for n in range(4):
            stage2(n, d).wait_send()
            stage3(n, d).wait_send()
    for p in range(6):
        up(p).wait_send()
        down(p).wait_send()
    for n in range(16):
        to_sibling(n).wait_send()
    for axis in range(2):
        for s in range(2):
            for way in range(2):
                first(axis, s, way).wait_send()
                second(axis, s, way).wait_send()
    for n in range(4):
        axis, s = PIECES[n]
        start = (axis * 2 + s) * SUB
        to_pair(n).wait_send()
        to_across(n).wait_send()
        pltpu.make_async_copy(newmom.at[n], newmom_hbm.at[:, pl.ds(start, SUB)], out_sem.at[0, n]).wait()
        pltpu.make_async_copy(update.at[n], update_hbm.at[:, pl.ds(start, SUB)], out_sem.at[1, n]).wait()
    for k in range(8):
        grads_out(k, 0).wait()
        grads_out(k, 1).wait()


def cosine_pair():
    freq = np.arange(SPAN)[:, None]
    place = np.arange(SPAN)[None, :]
    table = np.cos(np.pi * (place + 0.5) * freq / SPAN) * np.where(
        freq == 0, np.sqrt(1.0 / SPAN), np.sqrt(2.0 / SPAN)
    )
    inverse = np.kron(np.eye(2), table)
    return np.ascontiguousarray(inverse.T).astype(np.float32), inverse.astype(np.float32)


def local(head_out, gate_in, cotangent, momentum, chosen_index, out_weight, norm_gain):
    forward, inverse = cosine_pair()
    anywhere = pl.BlockSpec(memory_space=pl.ANY)
    vmem = pl.BlockSpec(memory_space=pltpu.VMEM)
    dma = pltpu.SemaphoreType.DMA
    scratch = [
        pltpu.VMEM((TOK, WIDTH), BF16),
        pltpu.VMEM((TOK, WIDTH), BF16),
        pltpu.VMEM((TOK, WIDTH), BF16),
        pltpu.VMEM((ROWS, WIDTH), F32),
        pltpu.VMEM((ROWS, WIDTH // 4), jnp.int32),
        pltpu.VMEM((4, 4, 4, 2, 16, WIDTH), BF16),
        pltpu.VMEM((TOK, WIDTH), BF16),
        pltpu.VMEM((2, 4, SUB, TOK), BF16),
        pltpu.VMEM((2, SUB, 4 * TOK), BF16),
        pltpu.VMEM((2, 2, 4, TOK, SUB), BF16),
        pltpu.VMEM((4, 3, 128, SUB), BF16),
        pltpu.VMEM((4, 3, 128, SUB), BF16),
        pltpu.VMEM((4, 128, SUB), F32),
        pltpu.VMEM((4, 3, ROWS, SUB), F32),
        pltpu.VMEM((4, ROWS, SUB), F32),
        pltpu.VMEM((4, ROWS, SUB), F32),
        pltpu.VMEM((4, ROWS, SUB), F32),
        pltpu.VMEM((4, ROWS, SUB), F32),
        pltpu.VMEM((4, ROWS, SUB), F32),
        pltpu.VMEM((4, ROWS, SUB), F32),
        pltpu.VMEM((2, SUB, SUB), BF16),
        pltpu.VMEM((SUB, SUB), BF16),
        pltpu.VMEM((TOK, 256), F32),
        pltpu.VMEM((8, TOK, 256), BF16),
        pltpu.VMEM((8, TOK, 256), BF16),
        dma((10,)), dma((2,)), dma((4, 8)),
        dma((3,)), dma((3,)), dma((3,)), dma((3,)),
        dma((6,)), dma((6,)), dma((6,)), dma((6,)),
        dma((16,)), dma((16,)),
        dma((2, 2, 2)), dma((2, 2, 2)), dma((2, 2, 2)), dma((2, 2, 2)),
        dma((2, 3)), dma((2, 3)),
        dma((4, 3)), dma((4, 3)), dma((4, 3)), dma((4, 3)),
        dma((4,)), dma((4,)), dma((4,)), dma((4,)),
    ]
    head_grad, gate_grad, new_momentum, update = pl.pallas_call(
        kernel,
        name="demo_step",
        out_shape=(
            jax.ShapeDtypeStruct((TOK, WIDTH), BF16),
            jax.ShapeDtypeStruct((TOK, WIDTH), BF16),
            jax.ShapeDtypeStruct((ROWS, WIDTH), F32),
            jax.ShapeDtypeStruct((ROWS, WIDTH), F32),
        ),
        in_specs=[anywhere] * 6 + [vmem] * 3,
        out_specs=(anywhere,) * 4,
        scratch_shapes=scratch,
        compiler_params=pltpu.CompilerParams(
            collective_id=0, has_side_effects=True, vmem_limit_bytes=56 * 2**20
        ),
        cost_estimate=pl.CostEstimate(flops=14 * 10**9, bytes_accessed=9 * 10**6, transcendentals=10**6),
    )(
        head_out[0], gate_in[0], cotangent[0], momentum[0], chosen_index[0], out_weight,
        norm_gain.reshape(1, HDIM), jnp.asarray(forward), jnp.asarray(inverse),
    )
    return head_grad[None], gate_grad[None], new_momentum[None], update


def solution(mesh):
    rows = P("group", "fsdp", None)
    return jax.shard_map(
        local,
        mesh=mesh,
        in_specs=(rows, rows, rows, rows, rows, P("fsdp", None), P()),
        out_specs=(rows, rows, rows, P("fsdp", None)),
        check_vma=False,
    )
```

```python
import functools

import jax
import jax.numpy as jnp
import numpy as np
from jax import lax
from jax.experimental import pallas as pl
from jax.experimental.pallas import tpu as pltpu
from jax.sharding import PartitionSpec as P

MESH = pl.DeviceIdType.MESH
HIGHEST = lax.Precision.HIGHEST
F32 = jnp.float32
BF16 = jnp.bfloat16

SPAN = 64
KEEP = 16
HDIM = 128
TOK = 384
WIDTH = 2048
ROWS = 32
SUB = 512
EPS = 1e-06
DECAY = 0.999

PIECES = ((0, 0), (1, 0), (0, 1), (1, 1))

UP_ORDER = (0, 1, 3, 2, 0, 1)
DOWN_ORDER = (0, 3, 1, 2, 3, 2)


def remote(src, dst, send, recv, device):
    return pltpu.make_async_remote_copy(
        src_ref=src, dst_ref=dst, send_sem=send, recv_sem=recv, device_id=device, device_id_type=MESH
    )


def kernel(
    head_hbm, gate_hbm, cot_hbm, mom_hbm, idx_hbm, w_hbm, gain_ref, dct_ref, idct_ref,
    hgrad_hbm, ggrad_hbm, newmom_hbm, update_hbm,
    heads, gates, cot, mom, idx, w6, low, gsend, gt, cslot, p2s, p2r, q, p3s, p3r, dec, dec_r, pair, pair_r,
    newmom, update, perm, spread, hgrad, ggrad,
    load_sem, own_sem, out_sem,
    wx_s, wx_r, wy_s, wy_r, up_s, up_r, dn_s, dn_r, sib_s, sib_r,
    c1_s, c1_r, c2_s, c2_r, gt_s, gt_r, s2_s, s2_r, s3_s, s3_r, d_s, d_r, e_s, e_r,
):
    f = lax.axis_index("fsdp")
    g = lax.axis_index("group")
    y, z, x = f // 16, (f // 4) % 4, f % 4
    lo, core = g // 2, g % 2
    sibling = {"fsdp": f, "group": g + 1 - 2 * core}
    across = {"fsdp": f, "group": (g + 2) % 4}
    above = {"fsdp": y * 16 + ((z + lo) % 4) * 4 + x, "group": (g + 2) % 4}
    below = {"fsdp": y * 16 + ((z + 3 + lo) % 4) * 4 + x, "group": (g + 2) % 4}

    def at_x(d):
        return {"fsdp": y * 16 + z * 4 + (x + d) % 4, "group": g}

    def at_y(d):
        return {"fsdp": ((y + d) % 4) * 16 + z * 4 + x, "group": g}

    def at_z(d):
        return {"fsdp": y * 16 + ((z + d) % 4) * 4 + x, "group": g}

    along = (at_x, at_y)
    mine = (x, y)

    barrier = pltpu.get_barrier_semaphore()
    partners = [at(d) for at in (at_x, at_y, at_z) for d in (1, 2, 3)] + [sibling, above, below]
    for device in partners:
        pl.semaphore_signal(barrier, inc=1, device_id=device, device_id_type=MESH)
    pl.semaphore_wait(barrier, len(partners))

    def wx(d):
        half = w_hbm.at[pl.ds(pl.multiple_of(core * 16, 16), 16)]
        return remote(half, w6.at[y, z, x, core], wx_s.at[d - 1], wx_r.at[d - 1], at_x(d))

    def wy(d):
        part = w6.at[y, z, :, core]
        return remote(part, part, wy_s.at[d - 1], wy_r.at[d - 1], at_y(d))

    def up(p):
        part = w6.at[(y + UP_ORDER[p]) % 4, (z + 8 - p // 4 - 1 + lo) % 4, :, core]
        return remote(part, part, up_s.at[p], up_r.at[p], above)

    def down(p):
        part = w6.at[(y + DOWN_ORDER[p]) % 4, (z + p // 4 + lo) % 4, :, core]
        return remote(part, part, dn_s.at[p], dn_r.at[p], below)

    def to_sibling(n):
        if n < 4:
            part = w6.at[(y + n) % 4, z, :, core]
        elif n < 10:
            part = w6.at[(y + UP_ORDER[n - 4]) % 4, (z + 3 - (n - 4) // 4) % 4, :, core]
        else:
            part = w6.at[(y + DOWN_ORDER[n - 10]) % 4, (z + 1 + (n - 10) // 4) % 4, :, core]
        return remote(part, part, sib_s.at[n], sib_r.at[n], sibling)

    def first(axis, s, way):
        dst = cslot.at[axis, s, mine[axis]]
        src = dst if axis + s else cot_hbm.at[:, :SUB]
        return remote(src, dst, c1_s.at[axis, s, way], c1_r.at[axis, s, way], along[axis](1 + 2 * way))

    def second(axis, s, way):
        part = cslot.at[axis, s, (mine[axis] + 3 + 2 * way) % 4, pl.ds(way * (TOK // 2), TOK // 2)]
        return remote(part, part, c2_s.at[axis, s, way], c2_r.at[axis, s, way], along[axis](1 + 2 * way))

    def gated_to(axis, d):
        src = gsend.at[axis, (mine[axis] + d) % 4]
        dst = gt.at[axis, :, pl.ds(pl.multiple_of(mine[axis] * TOK, 128), TOK)]
        return remote(src, dst, gt_s.at[axis, d - 1], gt_r.at[axis, d - 1], along[axis](d))

    def own_gated(axis):
        src = gsend.at[axis, mine[axis]]
        dst = gt.at[axis, :, pl.ds(pl.multiple_of(mine[axis] * TOK, 128), TOK)]
        return pltpu.make_async_copy(src, dst, own_sem.at[axis])

    def stage2(n, d):
        return remote(
            p2s.at[n, d - 1], p2r.at[n, d - 1], s2_s.at[n, d - 1], s2_r.at[n, d - 1], along[1 - PIECES[n][0]](d)
        )

    def stage3(n, d):
        return remote(p3s.at[n, d - 1], p3r.at[n, d - 1], s3_s.at[n, d - 1], s3_r.at[n, d - 1], at_z(d))

    def to_pair(n):
        return remote(dec.at[n], dec_r.at[n], d_s.at[n], d_r.at[n], sibling)

    def to_across(n):
        return remote(pair.at[n], pair_r.at[n], e_s.at[n], e_r.at[n], across)

    loads = [
        pltpu.make_async_copy(head_hbm, heads, load_sem.at[0]),
        pltpu.make_async_copy(gate_hbm, gates, load_sem.at[1]),
        pltpu.make_async_copy(
            w_hbm.at[pl.ds(pl.multiple_of(core * 16, 16), 16)], w6.at[y, z, x, core], load_sem.at[2]
        ),
    ]
    for axis in range(2):
        for s in range(2):
            loads.append(
                pltpu.make_async_copy(
                    cot_hbm.at[:, pl.ds((axis * 2 + s) * SUB, SUB)],
                    cslot.at[axis, s, mine[axis]],
                    load_sem.at[3 + axis * 2 + s],
                )
            )
    loads += [
        pltpu.make_async_copy(cot_hbm, cot, load_sem.at[7]),
        pltpu.make_async_copy(mom_hbm, mom, load_sem.at[8]),
        pltpu.make_async_copy(idx_hbm, idx, load_sem.at[9]),
    ]
    for d in (1, 2, 3):
        wx(d).start()
    for load in loads[:3]:
        load.start()
    for way in range(2):
        first(0, 0, way).start()
    for load in loads[3:]:
        load.start()

    row = lax.broadcasted_iota(jnp.int32, (SUB, SUB), 0)
    col = lax.broadcasted_iota(jnp.int32, (SUB, SUB), 1)
    source = ((row >> 5) & 3) * 128 + (row >> 7) * 32 + (row & 31)
    perm[0] = jnp.where(source == col, 1.0, 0.0).astype(BF16)
    perm[1] = jnp.where(row == col, 1.0, 0.0).astype(BF16)
    quarter, block = row >> 7, (row >> 4) & 7
    spread[...] = jnp.where((block == (col >> 6)) & (quarter == ((col >> 4) & 3)), 1.0, 0.0).astype(BF16)

    gain = gain_ref[...]
    loads[0].wait()
    loads[1].wait()

    def gated_rows(i, carry):
        rows = pl.ds(pl.multiple_of(i * 32, 32), 32)
        for k in range(WIDTH // HDIM):
            cols = slice(k * HDIM, (k + 1) * HDIM)
            h = heads[rows, cols].astype(F32)
            a = gates[rows, cols].astype(F32)
            n = h * lax.rsqrt(jnp.mean(h * h, axis=-1, keepdims=True) + EPS)
            low[rows, cols] = ((n * gain) * (a * jax.nn.sigmoid(a))).astype(BF16)
        return carry

    lax.fori_loop(0, 3, gated_rows, 0)

    for load in loads[2:]:
        load.wait()
    for d in (1, 2, 3):
        wx(d).wait_recv()
    for d in (1, 3, 2):
        wy(d).start()
    for way in range(2):
        first(1, 0, way).start()

    @pl.when(lo == 1)
    def _():
        up(0).start()

    @pl.when(lo == 0)
    def _():
        down(0).start()

    to_sibling(0).start()

    lax.fori_loop(3, 12, gated_rows, 0)

    for axis in range(2):

        def turn(b, carry, axis=axis):
            part = low[:, pl.ds(pl.multiple_of(b * SUB, SUB), SUB)]
            out = lax.dot_general(
                perm[axis], part, (((1,), (1,)), ((), ())), preferred_element_type=F32
            ).astype(BF16)
            if axis == 0:
                for to in range(4):
                    gsend[0, to, pl.ds(pl.multiple_of(b * 128, 128), 128), :] = out[to * 128 : (to + 1) * 128]
            else:
                gsend[1, b] = out
            return carry

        lax.fori_loop(0, 4, turn, 0)
        for d in (2, 1, 3):
            gated_to(axis, d).start()
        own_gated(axis).start()

    def relay(p):
        @pl.when(lo == 0)
        def _():
            up(p).wait_recv()
            up(p).start()
            to_sibling(4 + p).start()

        @pl.when(lo == 1)
        def _():
            down(p).wait_recv()
            down(p).start()
            to_sibling(10 + p).start()

    def follow(p):
        @pl.when(lo == 0)
        def _():
            down(p).wait_recv()
            if p in (1, 3):
                down(p // 2 + 4).start()
            to_sibling(10 + p).start()

        @pl.when(lo == 1)
        def _():
            up(p).wait_recv()
            if p < 2:
                up(p + 4).start()
            to_sibling(4 + p).start()

    def terms(n):
        axis, s = PIECES[n]
        right = cslot.at[axis, s]
        for d in (2, 1, 3, 0):
            owner = (mine[1 - axis] + d) % 4
            if axis == 0:
                left = gt[0, pl.ds(pl.multiple_of(owner * 128, 128), 128), :]
            else:
                left = jnp.concatenate(
                    [gt[1, pl.ds(pl.multiple_of(k * 128 + owner * 32, 32), 32), :] for k in range(4)], axis=0
                )
            part = jnp.dot(left, right[...].reshape(4 * TOK, SUB), preferred_element_type=F32)
            if d:
                p2s[n, d - 1] = part.astype(BF16)
                stage2(n, d).start()
            else:
                q[n] = part

    def pass_second(axis, s):
        for way in range(2):
            first(axis, s, way).wait_recv()
            second(axis, s, way).start()

    def own_piece(j):
        @pl.when(lo == 1)
        def _():
            up(UP_ORDER.index(j)).start()

        @pl.when(lo == 0)
        def _():
            down(DOWN_ORDER.index(j)).start()

        to_sibling(j).start()

    def second_in(axis, s):
        for way in range(2):
            second(axis, s, way).wait_recv()

    def sum2(n):
        for d in (1, 2, 3):
            stage2(n, d).wait_recv()
        q[n] += (p2r[n, 0].astype(F32) + p2r[n, 1].astype(F32)) + p2r[n, 2].astype(F32)
        for d in (2, 1, 3):
            rows = pl.ds(pl.multiple_of(((z + d) % 4) * ROWS, ROWS), ROWS)
            p3s[n, d - 1] = q[n, rows, :].astype(BF16)
            stage3(n, d).start()

    def gated_in(axis):
        own_gated(axis).wait()
        for d in (1, 2, 3):
            gated_to(axis, d).wait_recv()

    def moment_step(n):
        axis, s = PIECES[n]
        start = (axis * 2 + s) * SUB
        for d in (1, 2, 3):
            stage3(n, d).wait_recv()
        own = q[n, pl.ds(pl.multiple_of(z * ROWS, ROWS), ROWS), :]
        gradient = (own + p3r[n, 0].astype(F32)) + (p3r[n, 1].astype(F32) + p3r[n, 2].astype(F32))
        moment = DECAY * mom[:, start : start + SUB] + gradient * ((TOK * 64) ** -0.5)
        where = idx[:, start // 4 : start // 4 + 128]
        bits = jnp.left_shift(jnp.ones_like(where), where & 15)
        bits = jnp.concatenate(
            [jnp.where((where >> 4) == k, bits, 0).astype(F32).astype(BF16) for k in range(4)], axis=1
        )
        words = jnp.dot(bits, spread[...], preferred_element_type=F32).astype(jnp.int32)
        lane = lax.broadcasted_iota(jnp.int32, (ROWS, SUB), 1)
        chosen = (lax.shift_right_logical(words, lane & 15) & 1).astype(F32)

        def stacked(v):
            return jnp.concatenate([v[:, k * 128 : (k + 1) * 128] for k in range(4)], axis=0)

        coeffs = jnp.dot(stacked(moment), dct_ref[...], precision=HIGHEST, preferred_element_type=F32)
        decoded = jnp.dot(
            coeffs * stacked(chosen), idct_ref[...], precision=HIGHEST, preferred_element_type=F32
        )
        decoded = jnp.concatenate([decoded[k * ROWS : (k + 1) * ROWS] for k in range(4)], axis=1)
        dec[n] = decoded
        to_pair(n).start()
        newmom[n] = moment - decoded
        pltpu.make_async_copy(newmom.at[n], newmom_hbm.at[:, pl.ds(start, SUB)], out_sem.at[0, n]).start()

    def pair_step(n):
        to_pair(n).wait_recv()
        pair[n] = dec[n] + dec_r[n]
        to_across(n).start()

    def update_step(n):
        axis, s = PIECES[n]
        to_across(n).wait_recv()
        update[n] = (pair[n] + pair_r[n]) * 0.25
        start = (axis * 2 + s) * SUB
        pltpu.make_async_copy(update.at[n], update_hbm.at[:, pl.ds(start, SUB)], out_sem.at[1, n]).start()

    def grads_out(which, head):
        cols = pl.ds(pl.multiple_of(head * HDIM, HDIM), HDIM)
        src, dst = ((hgrad, hgrad_hbm), (ggrad, ggrad_hbm))[which]
        return pltpu.make_async_copy(src.at[:, cols], dst.at[:, cols], out_sem.at[2 + which, head])

    def back(block, pieces, arrivals):
        for n in arrivals:
            to_sibling(n).wait_recv()
        ys = [(y + j) % 4 for j in pieces]

        def back_rows(i, carry):
            rows = pl.ds(pl.multiple_of(i * 128, 128), 128)
            weight = jnp.concatenate([w6[v, block].reshape(HDIM, WIDTH) for v in ys], axis=0)
            both = lax.dot_general(
                cot[rows, :], weight, (((1,), (1,)), ((), ())), preferred_element_type=F32
            )
            for part in range(2):
                cols = pl.ds(pl.multiple_of((ys[part] * 4 + block) * HDIM, HDIM), HDIM)
                u = both[:, part * HDIM : (part + 1) * HDIM]
                h = heads[rows, cols].astype(F32)
                a = gates[rows, cols].astype(F32)
                r = lax.rsqrt(jnp.mean(h * h, axis=-1, keepdims=True) + EPS)
                n = h * r
                sig = jax.nn.sigmoid(a)
                ggrad[rows, cols] = ((u * (n * gain)) * (sig * (1.0 + a * (1.0 - sig)))).astype(BF16)
                ds = (u * (a * sig)) * gain
                hgrad[rows, cols] = (r * (ds - n * jnp.mean(ds * n, axis=-1, keepdims=True))).astype(BF16)
            return carry

        lax.fori_loop(0, TOK // 128, back_rows, 0)
        for v in ys:
            grads_out(0, v * 4 + block).start()
            grads_out(1, v * 4 + block).start()

    prev, prev2, after = (z + 3) % 4, (z + 2) % 4, (z + 1) % 4

    relay(0)
    for j in (1, 3):
        wy(4 - j).wait_recv()
        own_piece(j)
    pass_second(0, 0)
    for way in range(2):
        first(0, 1, way).start()
    wy(2).wait_recv()
    own_piece(2)
    follow(0)
    back(z, (0, 1), (0, 1))
    relay(1)
    pass_second(1, 0)
    for way in range(2):
        first(1, 1, way).start()
    back(z, (2, 3), (2, 3))
    relay(2)
    follow(1)
    gated_in(0)
    second_in(0, 0)
    terms(0)
    relay(3)
    follow(2)
    back(prev, (0, 1), (4, 5))
    relay(4)
    follow(3)
    pass_second(0, 1)
    gated_in(1)
    second_in(1, 0)
    terms(1)
    relay(5)
    follow(4)
    back(after, (2, 3), (11, 13))
    pass_second(1, 1)
    second_in(0, 1)
    terms(2)
    follow(5)
    sum2(1)
    back(prev, (2, 3), (6, 7))
    sum2(0)
    back(after, (0, 1), (10, 12))
    moment_step(1)
    second_in(1, 1)
    terms(3)
    moment_step(0)
    pair_step(1)
    back(prev2, (0, 1), (8, 9))
    pair_step(0)
    sum2(2)
    sum2(3)
    update_step(0)
    update_step(1)
    back(prev2, (2, 3), (14, 15))
    moment_step(2)
    moment_step(3)
    pair_step(2)
    pair_step(3)
    update_step(2)
    update_step(3)

    for d in (1, 2, 3):
        wx(d).wait_send()
        wy(d).wait_send()
        for axis in range(2):
            gated_to(axis, d).wait_send()
        for n in range(4):
            stage2(n, d).wait_send()
            stage3(n, d).wait_send()
    for p in range(6):
        up(p).wait_send()
        down(p).wait_send()
    for n in range(16):
        to_sibling(n).wait_send()
    for axis in range(2):
        for s in range(2):
            for way in range(2):
                first(axis, s, way).wait_send()
                second(axis, s, way).wait_send()
    for n in range(4):
        axis, s = PIECES[n]
        start = (axis * 2 + s) * SUB
        to_pair(n).wait_send()
        to_across(n).wait_send()
        pltpu.make_async_copy(newmom.at[n], newmom_hbm.at[:, pl.ds(start, SUB)], out_sem.at[0, n]).wait()
        pltpu.make_async_copy(update.at[n], update_hbm.at[:, pl.ds(start, SUB)], out_sem.at[1, n]).wait()
    for head in range(16):
        grads_out(0, head).wait()
        grads_out(1, head).wait()


def cosine_pair():
    freq = np.arange(SPAN)[:, None]
    place = np.arange(SPAN)[None, :]
    table = np.cos(np.pi * (place + 0.5) * freq / SPAN) * np.where(
        freq == 0, np.sqrt(1.0 / SPAN), np.sqrt(2.0 / SPAN)
    )
    inverse = np.kron(np.eye(2), table)
    return np.ascontiguousarray(inverse.T).astype(np.float32), inverse.astype(np.float32)


def local(head_out, gate_in, cotangent, momentum, chosen_index, out_weight, norm_gain):
    forward, inverse = cosine_pair()
    anywhere = pl.BlockSpec(memory_space=pl.ANY)
    vmem = pl.BlockSpec(memory_space=pltpu.VMEM)
    dma = pltpu.SemaphoreType.DMA
    scratch = [
        pltpu.VMEM((TOK, WIDTH), BF16),
        pltpu.VMEM((TOK, WIDTH), BF16),
        pltpu.VMEM((TOK, WIDTH), BF16),
        pltpu.VMEM((ROWS, WIDTH), F32),
        pltpu.VMEM((ROWS, WIDTH // 4), jnp.int32),
        pltpu.VMEM((4, 4, 4, 2, 16, WIDTH), BF16),
        pltpu.VMEM((TOK, WIDTH), BF16),
        pltpu.VMEM((2, 4, SUB, TOK), BF16),
        pltpu.VMEM((2, SUB, 4 * TOK), BF16),
        pltpu.VMEM((2, 2, 4, TOK, SUB), BF16),
        pltpu.VMEM((4, 3, 128, SUB), BF16),
        pltpu.VMEM((4, 3, 128, SUB), BF16),
        pltpu.VMEM((4, 128, SUB), F32),
        pltpu.VMEM((4, 3, ROWS, SUB), BF16),
        pltpu.VMEM((4, 3, ROWS, SUB), BF16),
        pltpu.VMEM((4, ROWS, SUB), F32),
        pltpu.VMEM((4, ROWS, SUB), F32),
        pltpu.VMEM((4, ROWS, SUB), F32),
        pltpu.VMEM((4, ROWS, SUB), F32),
        pltpu.VMEM((4, ROWS, SUB), F32),
        pltpu.VMEM((4, ROWS, SUB), F32),
        pltpu.VMEM((2, SUB, SUB), BF16),
        pltpu.VMEM((SUB, SUB), BF16),
        pltpu.VMEM((TOK, WIDTH), BF16),
        pltpu.VMEM((TOK, WIDTH), BF16),
        dma((10,)), dma((2,)), dma((4, 16)),
        dma((3,)), dma((3,)), dma((3,)), dma((3,)),
        dma((6,)), dma((6,)), dma((6,)), dma((6,)),
        dma((16,)), dma((16,)),
        dma((2, 2, 2)), dma((2, 2, 2)), dma((2, 2, 2)), dma((2, 2, 2)),
        dma((2, 3)), dma((2, 3)),
        dma((4, 3)), dma((4, 3)), dma((4, 3)), dma((4, 3)),
        dma((4,)), dma((4,)), dma((4,)), dma((4,)),
    ]
    head_grad, gate_grad, new_momentum, update = pl.pallas_call(
        kernel,
        name="demo_step",
        out_shape=(
            jax.ShapeDtypeStruct((TOK, WIDTH), BF16),
            jax.ShapeDtypeStruct((TOK, WIDTH), BF16),
            jax.ShapeDtypeStruct((ROWS, WIDTH), F32),
            jax.ShapeDtypeStruct((ROWS, WIDTH), F32),
        ),
        in_specs=[anywhere] * 6 + [vmem] * 3,
        out_specs=(anywhere,) * 4,
        scratch_shapes=scratch,
        compiler_params=pltpu.CompilerParams(
            collective_id=0, has_side_effects=True, vmem_limit_bytes=56 * 2**20
        ),
        cost_estimate=pl.CostEstimate(flops=14 * 10**9, bytes_accessed=9 * 10**6, transcendentals=10**6),
    )(
        head_out[0], gate_in[0], cotangent[0], momentum[0], chosen_index[0], out_weight,
        norm_gain.reshape(1, HDIM), jnp.asarray(forward), jnp.asarray(inverse),
    )
    return head_grad[None], gate_grad[None], new_momentum[None], update


def solution(mesh):
    rows = P("group", "fsdp", None)
    return jax.shard_map(
        local,
        mesh=mesh,
        in_specs=(rows, rows, rows, rows, rows, P("fsdp", None), P()),
        out_specs=(rows, rows, rows, P("fsdp", None)),
        check_vma=False,
    )
```

```python
import functools

import jax
import jax.numpy as jnp
import numpy as np
from jax import lax
from jax.experimental import pallas as pl
from jax.experimental.pallas import tpu as pltpu
from jax.sharding import PartitionSpec as P

MESH = pl.DeviceIdType.MESH
HIGHEST = lax.Precision.HIGHEST
F32 = jnp.float32
BF16 = jnp.bfloat16

SPAN = 64
KEEP = 16
HDIM = 128
TOK = 384
WIDTH = 2048
ROWS = 32
SUB = 512
EPS = 1e-06
DECAY = 0.999

PIECES = ((0, 0), (1, 0), (0, 1), (1, 1))

UP_ORDER = (0, 1, 3, 2, 0, 1)
DOWN_ORDER = (0, 3, 1, 2, 3, 2)


def remote(src, dst, send, recv, device):
    return pltpu.make_async_remote_copy(
        src_ref=src, dst_ref=dst, send_sem=send, recv_sem=recv, device_id=device, device_id_type=MESH
    )


def kernel(
    head_hbm, gate_hbm, cot_hbm, mom_hbm, idx_hbm, w_hbm, gain_ref, dct_ref, idct_ref,
    hgrad, ggrad, newmom, update,
    heads, gates, cot, mom, idx, w6, gsend, gt, cslot, p2s, p2r, q, p3s, p3r, dec, dec_r, pair, pair_r,
    spread,
    load_sem, own_sem,
    wx_s, wx_r, wy_s, wy_r, up_s, up_r, dn_s, dn_r, sib_s, sib_r,
    c1_s, c1_r, c2_s, c2_r, gt_s, gt_r, s2_s, s2_r, s3_s, s3_r, d_s, d_r, e_s, e_r,
):
    f = lax.axis_index("fsdp")
    g = lax.axis_index("group")
    y, z, x = f // 16, (f // 4) % 4, f % 4
    lo, core = g // 2, g % 2
    sibling = {"fsdp": f, "group": g + 1 - 2 * core}
    across = {"fsdp": f, "group": (g + 2) % 4}
    above = {"fsdp": y * 16 + ((z + lo) % 4) * 4 + x, "group": (g + 2) % 4}
    below = {"fsdp": y * 16 + ((z + 3 + lo) % 4) * 4 + x, "group": (g + 2) % 4}

    def at_x(d):
        return {"fsdp": y * 16 + z * 4 + (x + d) % 4, "group": g}

    def at_y(d):
        return {"fsdp": ((y + d) % 4) * 16 + z * 4 + x, "group": g}

    def at_z(d):
        return {"fsdp": y * 16 + ((z + d) % 4) * 4 + x, "group": g}

    along = (at_x, at_y)
    mine = (x, y)

    barrier = pltpu.get_barrier_semaphore()
    partners = [at(d) for at in (at_x, at_y, at_z) for d in (1, 2, 3)] + [sibling, above, below]
    for device in partners:
        pl.semaphore_signal(barrier, inc=1, device_id=device, device_id_type=MESH)
    pl.semaphore_wait(barrier, len(partners))

    def wx(d):
        half = w_hbm.at[pl.ds(pl.multiple_of(core * 16, 16), 16)]
        return remote(half, w6.at[y, z, x, core], wx_s.at[d - 1], wx_r.at[d - 1], at_x(d))

    def wy(d):
        part = w6.at[y, z, :, core]
        return remote(part, part, wy_s.at[d - 1], wy_r.at[d - 1], at_y(d))

    def up(p):
        part = w6.at[(y + UP_ORDER[p]) % 4, (z + 8 - p // 4 - 1 + lo) % 4, :, core]
        return remote(part, part, up_s.at[p], up_r.at[p], above)

    def down(p):
        part = w6.at[(y + DOWN_ORDER[p]) % 4, (z + p // 4 + lo) % 4, :, core]
        return remote(part, part, dn_s.at[p], dn_r.at[p], below)

    def to_sibling(n):
        if n < 4:
            part = w6.at[(y + n) % 4, z, :, core]
        elif n < 10:
            part = w6.at[(y + UP_ORDER[n - 4]) % 4, (z + 3 - (n - 4) // 4) % 4, :, core]
        else:
            part = w6.at[(y + DOWN_ORDER[n - 10]) % 4, (z + 1 + (n - 10) // 4) % 4, :, core]
        return remote(part, part, sib_s.at[n], sib_r.at[n], sibling)

    def first(axis, s, way, half):
        rows = pl.ds(half * (TOK // 2), TOK // 2)
        dst = cslot.at[axis, s, mine[axis], rows]
        src = dst if s else cot_hbm.at[rows, pl.ds(axis * 2 * SUB, SUB)]
        sems = axis, s, way, half
        return remote(src, dst, c1_s.at[sems], c1_r.at[sems], along[axis](1 + 2 * way))

    def second(axis, s, way):
        part = cslot.at[axis, s, (mine[axis] + 3 + 2 * way) % 4, pl.ds(way * (TOK // 2), TOK // 2)]
        return remote(part, part, c2_s.at[axis, s, way], c2_r.at[axis, s, way], along[axis](1 + 2 * way))

    def gated_to(axis, d):
        src = gsend.at[axis, (mine[axis] + d) % 4]
        dst = gt.at[axis, :, pl.ds(pl.multiple_of(mine[axis] * TOK, 128), TOK)]
        return remote(src, dst, gt_s.at[axis, d - 1], gt_r.at[axis, d - 1], along[axis](d))

    def own_gated(axis):
        src = gsend.at[axis, mine[axis]]
        dst = gt.at[axis, :, pl.ds(pl.multiple_of(mine[axis] * TOK, 128), TOK)]
        return pltpu.make_async_copy(src, dst, own_sem.at[axis])

    def stage2(n, d):
        return remote(
            p2s.at[n, d - 1], p2r.at[n, d - 1], s2_s.at[n, d - 1], s2_r.at[n, d - 1], along[1 - PIECES[n][0]](d)
        )

    def stage3(n, d):
        return remote(p3s.at[n, d - 1], p3r.at[n, d - 1], s3_s.at[n, d - 1], s3_r.at[n, d - 1], at_z(d))

    def to_pair(n):
        return remote(dec.at[n], dec_r.at[n], d_s.at[n], d_r.at[n], sibling)

    def to_across(n):
        return remote(pair.at[n], pair_r.at[n], e_s.at[n], e_r.at[n], across)

    loads = [
        pltpu.make_async_copy(head_hbm, heads, load_sem.at[0]),
        pltpu.make_async_copy(gate_hbm, gates, load_sem.at[1]),
        pltpu.make_async_copy(
            w_hbm.at[pl.ds(pl.multiple_of(core * 16, 16), 16)], w6.at[y, z, x, core], load_sem.at[2]
        ),
    ]
    for axis in range(2):
        for s in range(2):
            loads.append(
                pltpu.make_async_copy(
                    cot_hbm.at[:, pl.ds((axis * 2 + s) * SUB, SUB)],
                    cslot.at[axis, s, mine[axis]],
                    load_sem.at[3 + axis * 2 + s],
                )
            )
    loads += [
        pltpu.make_async_copy(cot_hbm, cot, load_sem.at[7]),
        pltpu.make_async_copy(mom_hbm, mom, load_sem.at[8]),
        pltpu.make_async_copy(idx_hbm, idx, load_sem.at[9]),
    ]
    for d in (1, 2, 3):
        wx(d).start()
    for load in loads[:3]:
        load.start()
    for way in range(2):
        first(0, 0, way, way).start()
        first(1, 0, way, way).start()
    for way in range(2):
        first(0, 0, way, 1 - way).start()
    for load in loads[3:]:
        load.start()

    row = lax.broadcasted_iota(jnp.int32, (SUB, SUB), 0)
    col = lax.broadcasted_iota(jnp.int32, (SUB, SUB), 1)
    quarter, block = row >> 7, (row >> 4) & 7
    spread[...] = jnp.where((block == (col >> 6)) & (quarter == ((col >> 4) & 3)), 1.0, 0.0).astype(BF16)

    gain = gain_ref[...]
    loads[0].wait()
    loads[1].wait()

    def gated_block(b, carry):
        for k in range(4):
            cols = pl.ds(pl.multiple_of(b * SUB + k * HDIM, HDIM), HDIM)
            h = heads[:, cols].astype(F32)
            a = gates[:, cols].astype(F32)
            n = h * lax.rsqrt(jnp.mean(h * h, axis=-1, keepdims=True) + EPS)
            low = ((n * gain) * (a * jax.nn.sigmoid(a))).astype(BF16)
            turned = low.T
            gsend[1, b, k * 128 : (k + 1) * 128, :] = turned
            for to in range(4):
                rows = pl.ds(pl.multiple_of(b * 128 + k * 32, 32), 32)
                gsend[0, to, rows, :] = turned[to * 32 : (to + 1) * 32]
        return carry

    lax.fori_loop(0, 1, gated_block, 0)

    for load in loads[2:]:
        load.wait()
    for d in (1, 2, 3):
        wx(d).wait_recv()
    for d in (1, 3, 2):
        wy(d).start()
    for way in range(2):
        first(1, 0, way, 1 - way).start()

    @pl.when(lo == 1)
    def _():
        up(0).start()

    @pl.when(lo == 0)
    def _():
        down(0).start()

    to_sibling(0).start()

    lax.fori_loop(1, 4, gated_block, 0)
    for d in (2, 1, 3):
        for axis in range(2):
            gated_to(axis, d).start()
    for axis in range(2):
        own_gated(axis).start()

    def relay(p):
        @pl.when(lo == 0)
        def _():
            up(p).wait_recv()
            up(p).start()
            to_sibling(4 + p).start()

        @pl.when(lo == 1)
        def _():
            down(p).wait_recv()
            down(p).start()
            to_sibling(10 + p).start()

    def follow(p):
        @pl.when(lo == 0)
        def _():
            down(p).wait_recv()
            if p in (1, 3):
                down(p // 2 + 4).start()
            to_sibling(10 + p).start()

        @pl.when(lo == 1)
        def _():
            up(p).wait_recv()
            if p < 2:
                up(p + 4).start()
            to_sibling(4 + p).start()

    def terms(n):
        axis, s = PIECES[n]
        owners = [(mine[1 - axis] + d) % 4 for d in (1, 2, 3, 0)]
        if axis == 0:
            starts = [owner * 128 for owner in owners]
            left = [gt[0, pl.ds(pl.multiple_of(v, 128), 128), :] for v in starts]
        else:
            starts = [k * 128 + owner * 32 for owner in owners for k in range(4)]
            left = [gt[1, pl.ds(pl.multiple_of(v, 32), 32), :] for v in starts]
        part = jnp.dot(
            jnp.concatenate(left, axis=0), cslot[axis, s].reshape(4 * TOK, SUB), preferred_element_type=F32
        )
        for d in (2, 1, 3):
            p2s[n, d - 1] = part[(d - 1) * 128 : d * 128].astype(BF16)
            stage2(n, d).start()
        q[n] = part[384:]

    def pass_second(axis, s):
        for way in range(2):
            first(axis, s, way, way).wait_recv()
            second(axis, s, way).start()

    def own_piece(j):
        @pl.when(lo == 1)
        def _():
            up(UP_ORDER.index(j)).start()

        @pl.when(lo == 0)
        def _():
            down(DOWN_ORDER.index(j)).start()

        to_sibling(j).start()

    def second_in(axis, s):
        for way in range(2):
            first(axis, s, way, 1 - way).wait_recv()
            second(axis, s, way).wait_recv()

    def sum2(n):
        for d in (1, 2, 3):
            stage2(n, d).wait_recv()
        q[n] += (p2r[n, 0].astype(F32) + p2r[n, 1].astype(F32)) + p2r[n, 2].astype(F32)
        for d in (2, 1, 3):
            rows = pl.ds(pl.multiple_of(((z + d) % 4) * ROWS, ROWS), ROWS)
            p3s[n, d - 1] = q[n, rows, :].astype(BF16)
            stage3(n, d).start()

    def gated_in(axis):
        own_gated(axis).wait()
        for d in (1, 2, 3):
            gated_to(axis, d).wait_recv()

    def moment_step(n):
        axis, s = PIECES[n]
        start = (axis * 2 + s) * SUB
        for d in (1, 2, 3):
            stage3(n, d).wait_recv()
        own = q[n, pl.ds(pl.multiple_of(z * ROWS, ROWS), ROWS), :]
        gradient = (own + p3r[n, 0].astype(F32)) + (p3r[n, 1].astype(F32) + p3r[n, 2].astype(F32))
        moment = DECAY * mom[:, start : start + SUB] + gradient * ((TOK * 64) ** -0.5)
        where = idx[:, start // 4 : start // 4 + 128]
        bits = jnp.left_shift(jnp.ones_like(where), where & 15)
        bits = jnp.concatenate(
            [jnp.where((where >> 4) == k, bits, 0).astype(F32).astype(BF16) for k in range(4)], axis=1
        )
        words = jnp.dot(bits, spread[...], preferred_element_type=F32).astype(jnp.int32)
        lane = lax.broadcasted_iota(jnp.int32, (ROWS, SUB), 1)
        chosen = (lax.shift_right_logical(words, lane & 15) & 1).astype(F32)

        def stacked(v):
            return jnp.concatenate([v[:, k * 128 : (k + 1) * 128] for k in range(4)], axis=0)

        coeffs = jnp.dot(stacked(moment), dct_ref[...], precision=HIGHEST, preferred_element_type=F32)
        decoded = jnp.dot(
            coeffs * stacked(chosen), idct_ref[...], precision=HIGHEST, preferred_element_type=F32
        )
        decoded = jnp.concatenate([decoded[k * ROWS : (k + 1) * ROWS] for k in range(4)], axis=1)
        dec[n] = decoded
        to_pair(n).start()
        newmom[:, start : start + SUB] = moment - decoded

    def pair_step(n):
        to_pair(n).wait_recv()
        pair[n] = dec[n] + dec_r[n]
        to_across(n).start()

    def update_step(n):
        axis, s = PIECES[n]
        to_across(n).wait_recv()
        start = (axis * 2 + s) * SUB
        update[:, start : start + SUB] = (pair[n] + pair_r[n]) * 0.25

    def back(block, pieces, arrivals):
        for n in arrivals:
            to_sibling(n).wait_recv()
        ys = [(y + j) % 4 for j in pieces]

        weight = jnp.concatenate([w6[v, block].reshape(HDIM, WIDTH) for v in ys], axis=0)
        both = lax.dot_general(cot[...], weight, (((1,), (1,)), ((), ())), preferred_element_type=F32)
        for part in range(2):
            head = ys[part] * 4 + block
            cols = pl.ds(pl.multiple_of(head * HDIM, HDIM), HDIM)
            u = both[:, part * HDIM : (part + 1) * HDIM]
            h = heads[:, cols].astype(F32)
            a = gates[:, cols].astype(F32)
            r = lax.rsqrt(jnp.mean(h * h, axis=-1, keepdims=True) + EPS)
            n = h * r
            sig = jax.nn.sigmoid(a)
            ggrad[:, cols] = ((u * (n * gain)) * (sig * (1.0 + a * (1.0 - sig)))).astype(BF16)
            ds = (u * (a * sig)) * gain
            hgrad[:, cols] = (r * (ds - n * jnp.mean(ds * n, axis=-1, keepdims=True))).astype(BF16)

    prev, prev2, after = (z + 3) % 4, (z + 2) % 4, (z + 1) % 4

    relay(0)
    for j in (1, 3):
        wy(4 - j).wait_recv()
        own_piece(j)
    pass_second(0, 0)
    for half in range(2):
        for way in range(2):
            first(0, 1, way, (way + half) % 2).start()
    wy(2).wait_recv()
    own_piece(2)
    follow(0)
    back(z, (0, 1), (0, 1))
    relay(1)
    pass_second(1, 0)
    for half in range(2):
        for way in range(2):
            first(1, 1, way, (way + half) % 2).start()
    back(z, (2, 3), (2, 3))
    relay(2)
    follow(1)
    gated_in(0)
    second_in(0, 0)
    terms(0)
    relay(3)
    follow(2)
    back(prev, (0, 1), (4, 5))
    relay(4)
    follow(3)
    pass_second(0, 1)
    gated_in(1)
    second_in(1, 0)
    terms(1)
    relay(5)
    follow(4)
    back(after, (2, 3), (11, 13))
    pass_second(1, 1)
    second_in(0, 1)
    terms(2)
    follow(5)
    sum2(1)
    back(prev, (2, 3), (6, 7))
    sum2(0)
    back(after, (0, 1), (10, 12))
    moment_step(1)
    second_in(1, 1)
    terms(3)
    moment_step(0)
    pair_step(1)
    back(prev2, (0, 1), (8, 9))
    pair_step(0)
    sum2(2)
    sum2(3)
    update_step(0)
    update_step(1)
    back(prev2, (2, 3), (14, 15))
    moment_step(2)
    moment_step(3)
    pair_step(2)
    pair_step(3)
    update_step(2)
    update_step(3)

    for d in (1, 2, 3):
        wx(d).wait_send()
        wy(d).wait_send()
        for axis in range(2):
            gated_to(axis, d).wait_send()
        for n in range(4):
            stage2(n, d).wait_send()
            stage3(n, d).wait_send()
    for p in range(6):
        up(p).wait_send()
        down(p).wait_send()
    for n in range(16):
        to_sibling(n).wait_send()
    for axis in range(2):
        for s in range(2):
            for way in range(2):
                first(axis, s, way, 0).wait_send()
                first(axis, s, way, 1).wait_send()
                second(axis, s, way).wait_send()
    for n in range(4):
        to_pair(n).wait_send()
        to_across(n).wait_send()


def place(*refs):
    sources, targets, sem = refs[:4], refs[4:8], refs[8]
    copies = []
    for n in range(4):
        rows = sources[n].shape[0] // 2
        for half in range(2):
            part = pl.ds(half * rows, rows)
            copies.append(
                pltpu.make_async_copy(sources[n].at[part], targets[n].at[part], sem.at[n * 2 + half])
            )
    for copy in copies:
        copy.start()
    for copy in copies:
        copy.wait()


def cosine_pair():
    freq = np.arange(SPAN)[:, None]
    place = np.arange(SPAN)[None, :]
    table = np.cos(np.pi * (place + 0.5) * freq / SPAN) * np.where(
        freq == 0, np.sqrt(1.0 / SPAN), np.sqrt(2.0 / SPAN)
    )
    inverse = np.kron(np.eye(2), table)
    return np.ascontiguousarray(inverse.T).astype(np.float32), inverse.astype(np.float32)


def local(head_out, gate_in, cotangent, momentum, chosen_index, out_weight, norm_gain):
    forward, inverse = cosine_pair()
    anywhere = pl.BlockSpec(memory_space=pl.ANY)
    vmem = pl.BlockSpec(memory_space=pltpu.VMEM)
    dma = pltpu.SemaphoreType.DMA
    scratch = [
        pltpu.VMEM((TOK, WIDTH), BF16),
        pltpu.VMEM((TOK, WIDTH), BF16),
        pltpu.VMEM((TOK, WIDTH), BF16),
        pltpu.VMEM((ROWS, WIDTH), F32),
        pltpu.VMEM((ROWS, WIDTH // 4), jnp.int32),
        pltpu.VMEM((4, 4, 4, 2, 16, WIDTH), BF16),
        pltpu.VMEM((2, 4, SUB, TOK), BF16),
        pltpu.VMEM((2, SUB, 4 * TOK), BF16),
        pltpu.VMEM((2, 2, 4, TOK, SUB), BF16),
        pltpu.VMEM((4, 3, 128, SUB), BF16),
        pltpu.VMEM((4, 3, 128, SUB), BF16),
        pltpu.VMEM((4, 128, SUB), F32),
        pltpu.VMEM((4, 3, ROWS, SUB), BF16),
        pltpu.VMEM((4, 3, ROWS, SUB), BF16),
        pltpu.VMEM((4, ROWS, SUB), F32),
        pltpu.VMEM((4, ROWS, SUB), F32),
        pltpu.VMEM((4, ROWS, SUB), F32),
        pltpu.VMEM((4, ROWS, SUB), F32),
        pltpu.VMEM((SUB, SUB), BF16),
        dma((10,)), dma((2,)),
        dma((3,)), dma((3,)), dma((3,)), dma((3,)),
        dma((6,)), dma((6,)), dma((6,)), dma((6,)),
        dma((16,)), dma((16,)),
        dma((2, 2, 2, 2)), dma((2, 2, 2, 2)), dma((2, 2, 2)), dma((2, 2, 2)),
        dma((2, 3)), dma((2, 3)),
        dma((4, 3)), dma((4, 3)), dma((4, 3)), dma((4, 3)),
        dma((4,)), dma((4,)), dma((4,)), dma((4,)),
    ]
    results = pl.pallas_call(
        kernel,
        name="demo_step",
        out_shape=(
            pltpu.VMEM((TOK, WIDTH), BF16),
            pltpu.VMEM((TOK, WIDTH), BF16),
            pltpu.VMEM((ROWS, WIDTH), F32),
            pltpu.VMEM((ROWS, WIDTH), F32),
        ),
        in_specs=[anywhere] * 6 + [vmem] * 3,
        out_specs=(vmem,) * 4,
        scratch_shapes=scratch,
        compiler_params=pltpu.CompilerParams(
            collective_id=0, has_side_effects=True, vmem_limit_bytes=60 * 2**20 + 2**18
        ),
        cost_estimate=pl.CostEstimate(flops=14 * 10**9, bytes_accessed=9 * 10**6, transcendentals=10**6),
    )(
        head_out[0], gate_in[0], cotangent[0], momentum[0], chosen_index[0], out_weight,
        norm_gain.reshape(1, HDIM), jnp.asarray(forward), jnp.asarray(inverse),
    )
    head_grad, gate_grad, new_momentum, update = pl.pallas_call(
        place,
        name="place_results",
        out_shape=tuple(jax.ShapeDtypeStruct(v.shape, v.dtype) for v in results),
        in_specs=[vmem] * 4,
        out_specs=(anywhere,) * 4,
        scratch_shapes=[dma((8,))],
        compiler_params=pltpu.CompilerParams(vmem_limit_bytes=2**20),
    )(*(pltpu.with_memory_space_constraint(v, pltpu.VMEM) for v in results))
    return head_grad[None], gate_grad[None], new_momentum[None], update


def solution(mesh):
    rows = P("group", "fsdp", None)
    return jax.shard_map(
        local,
        mesh=mesh,
        in_specs=(rows, rows, rows, rows, rows, P("fsdp", None), P()),
        out_specs=(rows, rows, rows, P("fsdp", None)),
        check_vma=False,
    )
```

```python
import functools

import jax
import jax.numpy as jnp
import numpy as np
from jax import lax
from jax.experimental import pallas as pl
from jax.experimental.pallas import tpu as pltpu
from jax.sharding import PartitionSpec as P

MESH = pl.DeviceIdType.MESH
HIGHEST = lax.Precision.HIGHEST
F32 = jnp.float32
BF16 = jnp.bfloat16

SPAN = 64
KEEP = 16
HDIM = 128
TOK = 384
WIDTH = 2048
ROWS = 32
SUB = 512
EPS = 1e-06
DECAY = 0.999

PIECES = ((0, 0), (1, 0), (0, 1), (1, 1))

UP_ORDER = (0, 1, 3, 2, 0, 1)
DOWN_ORDER = (0, 3, 1, 2, 3, 2)


def remote(src, dst, send, recv, device):
    return pltpu.make_async_remote_copy(
        src_ref=src, dst_ref=dst, send_sem=send, recv_sem=recv, device_id=device, device_id_type=MESH
    )


def kernel(
    head_hbm, gate_hbm, cot_hbm, mom_hbm, idx_hbm, w_hbm, gain_ref, dct_ref, idct_ref,
    hgrad, ggrad, newmom, update,
    heads, gates, cot, mom, idx, w6, gsend, gt, cslot, p2s, p2r, q, p3s, p3r, dec, dec_r, chosen,
    load_sem, own_sem,
    w1_s, w1_r, w2_s, w2_r, up_s, up_r, dn_s, dn_r, sib_s, sib_r,
    c1_s, c1_r, c2_s, c2_r, gt_s, gt_r, s2_s, s2_r, s3_s, s3_r, d_s, d_r,
):
    f = lax.axis_index("fsdp")
    g = lax.axis_index("group")
    y, z, x = f // 16, (f // 4) % 4, f % 4
    lo, core = g // 2, g % 2
    sibling = {"fsdp": f, "group": g + 1 - 2 * core}
    across = {"fsdp": f, "group": (g + 2) % 4}
    diagonal = {"fsdp": f, "group": 3 - g}
    above = {"fsdp": y * 16 + ((z + lo) % 4) * 4 + x, "group": (g + 2) % 4}
    below = {"fsdp": y * 16 + ((z + 3 + lo) % 4) * 4 + x, "group": (g + 2) % 4}

    def at_x(d):
        return {"fsdp": y * 16 + z * 4 + (x + d) % 4, "group": g}

    def at_y(d):
        return {"fsdp": ((y + d) % 4) * 16 + z * 4 + x, "group": g}

    def at_z(d):
        return {"fsdp": y * 16 + ((z + d) % 4) * 4 + x, "group": g}

    along = (at_x, at_y)
    mine = (x, y)

    outer = (1 - core) * y + core * x
    inner = (1 - core) * x + core * y

    def at_inner(d):
        return {"fsdp": (1 - core) * at_x(d)["fsdp"] + core * at_y(d)["fsdp"], "group": g}

    def at_outer(d):
        return {"fsdp": (1 - core) * at_y(d)["fsdp"] + core * at_x(d)["fsdp"], "group": g}

    def w1(d):
        half = w_hbm.at[pl.ds(pl.multiple_of(core * 16, 16), 16)]
        return remote(half, w6.at[outer, z, inner, core], w1_s.at[d - 1], w1_r.at[d - 1], at_inner(d))

    def w2(d):
        part = w6.at[outer, z, :, core]
        return remote(part, part, w2_s.at[d - 1], w2_r.at[d - 1], at_outer(d))

    def up(p):
        part = w6.at[(outer + UP_ORDER[p]) % 4, (z + 8 - p // 4 - 1 + lo) % 4, :, core]
        return remote(part, part, up_s.at[p], up_r.at[p], above)

    def down(p):
        part = w6.at[(outer + DOWN_ORDER[p]) % 4, (z + p // 4 + lo) % 4, :, core]
        return remote(part, part, dn_s.at[p], dn_r.at[p], below)

    def to_sibling(n):
        if n < 4:
            part = w6.at[(outer + n) % 4, z, :, core]
        elif n < 10:
            part = w6.at[(outer + UP_ORDER[n - 4]) % 4, (z + 3 - (n - 4) // 4) % 4, :, core]
        else:
            part = w6.at[(outer + DOWN_ORDER[n - 10]) % 4, (z + 1 + (n - 10) // 4) % 4, :, core]
        return remote(part, part, sib_s.at[n], sib_r.at[n], sibling)

    def first(axis, s, way, half):
        rows = pl.ds(half * (TOK // 2), TOK // 2)
        dst = cslot.at[axis, s, mine[axis], rows]
        src = dst if s else cot_hbm.at[rows, pl.ds(axis * 2 * SUB, SUB)]
        sems = axis, s, way, half
        return remote(src, dst, c1_s.at[sems], c1_r.at[sems], along[axis](1 + 2 * way))

    def second(axis, s, way):
        part = cslot.at[axis, s, (mine[axis] + 3 + 2 * way) % 4, pl.ds(way * (TOK // 2), TOK // 2)]
        return remote(part, part, c2_s.at[axis, s, way], c2_r.at[axis, s, way], along[axis](1 + 2 * way))

    def gated_to(axis, d):
        src = gsend.at[axis, (mine[axis] + d) % 4]
        dst = gt.at[axis, :, pl.ds(pl.multiple_of(mine[axis] * TOK, 128), TOK)]
        return remote(src, dst, gt_s.at[axis, d - 1], gt_r.at[axis, d - 1], along[axis](d))

    def own_gated(axis):
        src = gsend.at[axis, mine[axis]]
        dst = gt.at[axis, :, pl.ds(pl.multiple_of(mine[axis] * TOK, 128), TOK)]
        return pltpu.make_async_copy(src, dst, own_sem.at[axis])

    def stage2(n, d):
        return remote(
            p2s.at[n, d - 1], p2r.at[n, d - 1], s2_s.at[n, d - 1], s2_r.at[n, d - 1], along[1 - PIECES[n][0]](d)
        )

    def stage3(n, d):
        return remote(p3s.at[n, d - 1], p3r.at[n, d - 1], s3_s.at[n, d - 1], s3_r.at[n, d - 1], at_z(d))

    def exchange(n, way):
        device = (diagonal, across, sibling)[way]
        return remote(dec.at[n], dec_r.at[n, way], d_s.at[n, way], d_r.at[n, way], device)

    loads = [
        pltpu.make_async_copy(head_hbm, heads, load_sem.at[0]),
        pltpu.make_async_copy(gate_hbm, gates, load_sem.at[1]),
        pltpu.make_async_copy(
            w_hbm.at[pl.ds(pl.multiple_of(core * 16, 16), 16)], w6.at[outer, z, inner, core], load_sem.at[2]
        ),
    ]
    for axis in range(2):
        for s in range(2):
            loads.append(
                pltpu.make_async_copy(
                    cot_hbm.at[:, pl.ds((axis * 2 + s) * SUB, SUB)],
                    cslot.at[axis, s, mine[axis]],
                    load_sem.at[3 + axis * 2 + s],
                )
            )
    loads += [
        pltpu.make_async_copy(cot_hbm, cot, load_sem.at[7]),
        pltpu.make_async_copy(mom_hbm, mom, load_sem.at[8]),
        pltpu.make_async_copy(idx_hbm, idx, load_sem.at[9]),
    ]
    for load in loads:
        load.start()

    barrier = pltpu.get_barrier_semaphore()
    partners = [at(d) for at in (at_x, at_y, at_z) for d in (1, 2, 3)] + [sibling, diagonal, above, below]
    for device in partners:
        pl.semaphore_signal(barrier, inc=1, device_id=device, device_id_type=MESH)
    pl.semaphore_wait(barrier, len(partners))

    for d in (1, 2, 3):
        w1(d).start()
    for way in range(2):
        first(0, 0, way, way).start()
        first(1, 0, way, way).start()

    gain = gain_ref[...]
    loads[0].wait()
    loads[1].wait()

    def gated_block(b, carry):
        for k in range(4):
            cols = pl.ds(pl.multiple_of(b * SUB + k * HDIM, HDIM), HDIM)
            h = heads[:, cols].astype(F32)
            a = gates[:, cols].astype(F32)
            n = h * lax.rsqrt(jnp.mean(h * h, axis=-1, keepdims=True) + EPS)
            low = ((n * gain) * (a * jax.nn.sigmoid(a))).astype(BF16)
            turned = low.T
            gsend[1, b, k * 128 : (k + 1) * 128, :] = turned
            for to in range(4):
                rows = pl.ds(pl.multiple_of(b * 128 + k * 32, 32), 32)
                gsend[0, to, rows, :] = turned[to * 32 : (to + 1) * 32]
        return carry

    lax.fori_loop(0, 1, gated_block, 0)

    for load in loads[2:]:
        load.wait()
    for d in (1, 2, 3):
        w1(d).wait_recv()
    for d in (1, 3, 2):
        w2(d).start()
    @pl.when(lo == 1)
    def _():
        up(0).start()

    @pl.when(lo == 0)
    def _():
        down(0).start()

    to_sibling(0).start()

    lax.fori_loop(1, 4, gated_block, 0)
    for axis in range(2):
        own_gated(axis).start()

    def relay(p):
        @pl.when(lo == 0)
        def _():
            up(p).wait_recv()
            up(p).start()
            to_sibling(4 + p).start()

        @pl.when(lo == 1)
        def _():
            down(p).wait_recv()
            down(p).start()
            to_sibling(10 + p).start()

    def follow(p):
        @pl.when(lo == 0)
        def _():
            down(p).wait_recv()
            if p in (1, 3):
                down(p // 2 + 4).start()
            to_sibling(10 + p).start()

        @pl.when(lo == 1)
        def _():
            up(p).wait_recv()
            if p < 2:
                up(p + 4).start()
            to_sibling(4 + p).start()

    def terms(n):
        axis, s = PIECES[n]
        owners = [(mine[1 - axis] + d) % 4 for d in (1, 2, 3, 0)]
        if axis == 0:
            starts = [owner * 128 for owner in owners]
            left = [gt[0, pl.ds(pl.multiple_of(v, 128), 128), :] for v in starts]
        else:
            starts = [k * 128 + owner * 32 for owner in owners for k in range(4)]
            left = [gt[1, pl.ds(pl.multiple_of(v, 32), 32), :] for v in starts]
        part = jnp.dot(
            jnp.concatenate(left, axis=0), cslot[axis, s].reshape(4 * TOK, SUB), preferred_element_type=F32
        )
        for d in (2, 1, 3):
            p2s[n, d - 1] = part[(d - 1) * 128 : d * 128].astype(BF16)
            stage2(n, d).start()
        q[n] = part[384:]

    def pass_second(axis, s):
        for way in range(2):
            first(axis, s, way, way).wait_recv()
            second(axis, s, way).start()

    def own_piece(j):
        @pl.when(lo == 1)
        def _():
            up(UP_ORDER.index(j)).start()

        @pl.when(lo == 0)
        def _():
            down(DOWN_ORDER.index(j)).start()

        to_sibling(j).start()

    def second_in(axis, s):
        for way in range(2):
            first(axis, s, way, 1 - way).wait_recv()
            second(axis, s, way).wait_recv()

    def sum2(n):
        for d in (1, 2, 3):
            stage2(n, d).wait_recv()
        q[n] += (p2r[n, 0].astype(F32) + p2r[n, 1].astype(F32)) + p2r[n, 2].astype(F32)
        for d in (2, 1, 3):
            rows = pl.ds(pl.multiple_of(((z + d) % 4) * ROWS, ROWS), ROWS)
            p3s[n, d - 1] = q[n, rows, :].astype(BF16)
            stage3(n, d).start()

    def gated_in(axis):
        own_gated(axis).wait()
        for d in (1, 2, 3):
            gated_to(axis, d).wait_recv()

    def stacked(v):
        return jnp.concatenate([v[:, k * 128 : (k + 1) * 128] for k in range(4)], axis=0)

    def choose():
        row = lax.broadcasted_iota(jnp.int32, (SUB, SUB), 0)
        col = lax.broadcasted_iota(jnp.int32, (SUB, SUB), 1)
        same = (((row >> 4) & 7) == (col >> 6)) & ((row >> 7) == ((col >> 4) & 3))
        spread = jnp.where(same, 1.0, 0.0).astype(BF16)
        where = stacked(idx[...])
        bits = jnp.left_shift(jnp.ones_like(where), where & 15)
        bits = jnp.concatenate(
            [jnp.where((where >> 4) == k, bits, 0).astype(F32).astype(BF16) for k in range(4)], axis=1
        )
        words = jnp.dot(bits, spread, preferred_element_type=F32).astype(jnp.int32)
        lane = lax.broadcasted_iota(jnp.int32, (4 * ROWS, SUB), 1)
        kept = (lax.shift_right_logical(words, lane & 15) & 1).astype(F32)
        for n in range(4):
            axis, s = PIECES[n]
            piece = axis * 2 + s
            chosen[n] = stacked(kept[piece * ROWS : (piece + 1) * ROWS])

    def moment_step(n):
        axis, s = PIECES[n]
        start = (axis * 2 + s) * SUB
        for d in (1, 2, 3):
            stage3(n, d).wait_recv()
        own = q[n, pl.ds(pl.multiple_of(z * ROWS, ROWS), ROWS), :]
        gradient = (own + p3r[n, 0].astype(F32)) + (p3r[n, 1].astype(F32) + p3r[n, 2].astype(F32))
        moment = DECAY * mom[:, start : start + SUB] + gradient * ((TOK * 64) ** -0.5)
        coeffs = jnp.dot(stacked(moment), dct_ref[...], precision=HIGHEST, preferred_element_type=F32)
        decoded = jnp.dot(
            coeffs * chosen[n], idct_ref[...], precision=HIGHEST, preferred_element_type=F32
        )
        decoded = jnp.concatenate([decoded[k * ROWS : (k + 1) * ROWS] for k in range(4)], axis=1)
        dec[n] = decoded
        for way in range(3):
            exchange(n, way).start()
        newmom[:, start : start + SUB] = moment - decoded

    def update_step(n):
        axis, s = PIECES[n]
        start = (axis * 2 + s) * SUB
        for way in range(3):
            exchange(n, way).wait_recv()
        update[:, start : start + SUB] = ((dec[n] + dec_r[n, 2]) + (dec_r[n, 0] + dec_r[n, 1])) * 0.25

    def back(block, ys):
        halves = []
        for v in ys:
            for k in range(4):
                halves += [w6[v, block, k, 0], w6[k, block, v, 1]]
        weight = jnp.concatenate(halves, axis=0)
        both = lax.dot_general(cot[...], weight, (((1,), (1,)), ((), ())), preferred_element_type=F32)
        for part in range(len(ys)):
            head = ys[part] * 4 + block
            cols = pl.ds(pl.multiple_of(head * HDIM, HDIM), HDIM)
            u = both[:, part * HDIM : (part + 1) * HDIM]
            h = heads[:, cols].astype(F32)
            a = gates[:, cols].astype(F32)
            r = lax.rsqrt(jnp.mean(h * h, axis=-1, keepdims=True) + EPS)
            n = h * r
            sig = jax.nn.sigmoid(a)
            ggrad[:, cols] = ((u * (n * gain)) * (sig * (1.0 + a * (1.0 - sig)))).astype(BF16)
            ds = (u * (a * sig)) * gain
            hgrad[:, cols] = (r * (ds - n * jnp.mean(ds * n, axis=-1, keepdims=True))).astype(BF16)

    prev, prev2, after = (z + 3) % 4, (z + 2) % 4, (z + 1) % 4

    def block_back(block, arrivals):
        for n in arrivals:
            to_sibling(n).wait_recv()
        back(block, (0, 1))
        back(block, (2, 3))

    for way in range(2):
        first(0, 0, way, 1 - way).start()
        first(1, 0, way, 1 - way).start()
    for d in (2, 1, 3):
        for axis in range(2):
            gated_to(axis, d).start()
    for j in (1, 3):
        w2(4 - j).wait_recv()
        own_piece(j)
    w2(2).wait_recv()
    own_piece(2)
    pass_second(0, 0)
    pass_second(1, 0)
    for half in range(2):
        for way in range(2):
            first(0, 1, way, (way + half) % 2).start()
            first(1, 1, way, (way + half) % 2).start()
    relay(0)
    follow(0)
    choose()
    relay(1)
    block_back(z, range(4))
    relay(2)
    follow(1)
    relay(3)
    follow(2)
    relay(4)
    follow(3)
    gated_in(0)
    second_in(0, 0)
    terms(0)
    gated_in(1)
    second_in(1, 0)
    terms(1)
    relay(5)
    follow(4)
    block_back(prev, range(4, 8))
    pass_second(0, 1)
    pass_second(1, 1)
    block_back(after, range(10, 14))
    follow(5)
    sum2(0)
    sum2(1)
    second_in(0, 1)
    terms(2)
    second_in(1, 1)
    terms(3)
    moment_step(0)
    moment_step(1)
    block_back(prev2, (8, 9, 14, 15))
    sum2(2)
    sum2(3)
    update_step(0)
    update_step(1)
    moment_step(2)
    moment_step(3)
    update_step(2)
    update_step(3)

    for d in (1, 2, 3):
        w1(d).wait_send()
        w2(d).wait_send()
        for axis in range(2):
            gated_to(axis, d).wait_send()
        for n in range(4):
            stage2(n, d).wait_send()
            stage3(n, d).wait_send()
    for p in range(6):
        up(p).wait_send()
        down(p).wait_send()
    for n in range(16):
        to_sibling(n).wait_send()
    for axis in range(2):
        for s in range(2):
            for way in range(2):
                first(axis, s, way, 0).wait_send()
                first(axis, s, way, 1).wait_send()
                second(axis, s, way).wait_send()
    for n in range(4):
        for way in range(3):
            exchange(n, way).wait_send()


def place(*refs):
    sources, targets, sem = refs[:4], refs[4:8], refs[8]
    copies = []
    for n in range(4):
        rows = sources[n].shape[0] // 2
        for half in range(2):
            part = pl.ds(half * rows, rows)
            copies.append(
                pltpu.make_async_copy(sources[n].at[part], targets[n].at[part], sem.at[n * 2 + half])
            )
    for copy in copies:
        copy.start()
    for copy in copies:
        copy.wait()


def cosine_pair():
    freq = np.arange(SPAN)[:, None]
    place = np.arange(SPAN)[None, :]
    table = np.cos(np.pi * (place + 0.5) * freq / SPAN) * np.where(
        freq == 0, np.sqrt(1.0 / SPAN), np.sqrt(2.0 / SPAN)
    )
    inverse = np.kron(np.eye(2), table)
    return np.ascontiguousarray(inverse.T).astype(np.float32), inverse.astype(np.float32)


def local(head_out, gate_in, cotangent, momentum, chosen_index, out_weight, norm_gain):
    forward, inverse = cosine_pair()
    anywhere = pl.BlockSpec(memory_space=pl.ANY)
    vmem = pl.BlockSpec(memory_space=pltpu.VMEM)
    dma = pltpu.SemaphoreType.DMA
    scratch = [
        pltpu.VMEM((TOK, WIDTH), BF16),
        pltpu.VMEM((TOK, WIDTH), BF16),
        pltpu.VMEM((TOK, WIDTH), BF16),
        pltpu.VMEM((ROWS, WIDTH), F32),
        pltpu.VMEM((ROWS, WIDTH // 4), jnp.int32),
        pltpu.VMEM((4, 4, 4, 2, 16, WIDTH), BF16),
        pltpu.VMEM((2, 4, SUB, TOK), BF16),
        pltpu.VMEM((2, SUB, 4 * TOK), BF16),
        pltpu.VMEM((2, 2, 4, TOK, SUB), BF16),
        pltpu.VMEM((4, 3, 128, SUB), BF16),
        pltpu.VMEM((4, 3, 128, SUB), BF16),
        pltpu.VMEM((4, 128, SUB), F32),
        pltpu.VMEM((4, 3, ROWS, SUB), BF16),
        pltpu.VMEM((4, 3, ROWS, SUB), BF16),
        pltpu.VMEM((4, ROWS, SUB), F32),
        pltpu.VMEM((4, 3, ROWS, SUB), F32),
        pltpu.VMEM((4, 128, 128), F32),
        dma((10,)), dma((2,)),
        dma((3,)), dma((3,)), dma((3,)), dma((3,)),
        dma((6,)), dma((6,)), dma((6,)), dma((6,)),
        dma((16,)), dma((16,)),
        dma((2, 2, 2, 2)), dma((2, 2, 2, 2)), dma((2, 2, 2)), dma((2, 2, 2)),
        dma((2, 3)), dma((2, 3)),
        dma((4, 3)), dma((4, 3)), dma((4, 3)), dma((4, 3)),
        dma((4, 3)), dma((4, 3)),
    ]
    results = pl.pallas_call(
        kernel,
        name="demo_step",
        out_shape=(
            pltpu.VMEM((TOK, WIDTH), BF16),
            pltpu.VMEM((TOK, WIDTH), BF16),
            pltpu.VMEM((ROWS, WIDTH), F32),
            pltpu.VMEM((ROWS, WIDTH), F32),
        ),
        in_specs=[anywhere] * 6 + [vmem] * 3,
        out_specs=(vmem,) * 4,
        scratch_shapes=scratch,
        compiler_params=pltpu.CompilerParams(
            collective_id=0, has_side_effects=True, vmem_limit_bytes=60 * 2**20 + 2**18
        ),
        cost_estimate=pl.CostEstimate(flops=14 * 10**9, bytes_accessed=9 * 10**6, transcendentals=10**6),
    )(
        head_out[0], gate_in[0], cotangent[0], momentum[0], chosen_index[0], out_weight,
        norm_gain.reshape(1, HDIM), jnp.asarray(forward), jnp.asarray(inverse),
    )
    head_grad, gate_grad, new_momentum, update = pl.pallas_call(
        place,
        name="place_results",
        out_shape=tuple(jax.ShapeDtypeStruct(v.shape, v.dtype) for v in results),
        in_specs=[vmem] * 4,
        out_specs=(anywhere,) * 4,
        scratch_shapes=[dma((8,))],
        compiler_params=pltpu.CompilerParams(vmem_limit_bytes=2**20),
    )(*(pltpu.with_memory_space_constraint(v, pltpu.VMEM) for v in results))
    return head_grad[None], gate_grad[None], new_momentum[None], update


def solution(mesh):
    rows = P("group", "fsdp", None)
    return jax.shard_map(
        local,
        mesh=mesh,
        in_specs=(rows, rows, rows, rows, rows, P("fsdp", None), P()),
        out_specs=(rows, rows, rows, P("fsdp", None)),
        check_vma=False,
    )
```

```python
import functools

import jax
import jax.numpy as jnp
import numpy as np
from jax import lax
from jax.experimental import pallas as pl
from jax.experimental.pallas import tpu as pltpu
from jax.sharding import PartitionSpec as P

MESH = pl.DeviceIdType.MESH
HIGHEST = lax.Precision.HIGHEST
F32 = jnp.float32
BF16 = jnp.bfloat16

SPAN = 64
KEEP = 16
HDIM = 128
TOK = 384
WIDTH = 2048
ROWS = 32
SUB = 512
EPS = 1e-06
DECAY = 0.999

PIECES = ((0, 0), (1, 0), (0, 1), (1, 1))

UP_ORDER = (0, 1, 3, 2, 0, 1)
DOWN_ORDER = (0, 3, 1, 2, 3, 2)


def remote(src, dst, send, recv, device):
    return pltpu.make_async_remote_copy(
        src_ref=src, dst_ref=dst, send_sem=send, recv_sem=recv, device_id=device, device_id_type=MESH
    )


def kernel(
    head_hbm, gate_hbm, cot_hbm, mom_hbm, idx_hbm, w_hbm, gain_ref, dct_ref, idct_ref,
    hgrad, ggrad, newmom, update,
    heads, gates, cot, mom, idx, w6, gsend, gt, cslot, p2s, p2r, q, p3s, p3r, dec, dec_r, chosen,
    load_sem, own_sem,
    w1_s, w1_r, w2_s, w2_r, up_s, up_r, dn_s, dn_r, sib_s, sib_r,
    c1_s, c1_r, c2_s, c2_r, gt_s, gt_r, s2_s, s2_r, s3_s, s3_r, d_s, d_r,
):
    f = lax.axis_index("fsdp")
    g = lax.axis_index("group")
    y, z, x = f // 16, (f // 4) % 4, f % 4
    lo, core = g // 2, g % 2
    sibling = {"fsdp": f, "group": g + 1 - 2 * core}
    across = {"fsdp": f, "group": (g + 2) % 4}
    diagonal = {"fsdp": f, "group": 3 - g}
    above = {"fsdp": y * 16 + ((z + lo) % 4) * 4 + x, "group": (g + 2) % 4}
    below = {"fsdp": y * 16 + ((z + 3 + lo) % 4) * 4 + x, "group": (g + 2) % 4}

    def at_x(d):
        return {"fsdp": y * 16 + z * 4 + (x + d) % 4, "group": g}

    def at_y(d):
        return {"fsdp": ((y + d) % 4) * 16 + z * 4 + x, "group": g}

    def at_z(d):
        return {"fsdp": y * 16 + ((z + d) % 4) * 4 + x, "group": g}

    along = (at_x, at_y)
    mine = (x, y)

    outer = (1 - core) * y + core * x
    inner = (1 - core) * x + core * y

    def at_inner(d):
        return {"fsdp": (1 - core) * at_x(d)["fsdp"] + core * at_y(d)["fsdp"], "group": g}

    def at_outer(d):
        return {"fsdp": (1 - core) * at_y(d)["fsdp"] + core * at_x(d)["fsdp"], "group": g}

    def w1(d):
        half = w_hbm.at[pl.ds(pl.multiple_of(core * 16, 16), 16)]
        return remote(half, w6.at[outer, z, inner, core], w1_s.at[d - 1], w1_r.at[d - 1], at_inner(d))

    def w2(d):
        part = w6.at[outer, z, :, core]
        return remote(part, part, w2_s.at[d - 1], w2_r.at[d - 1], at_outer(d))

    def up(p):
        part = w6.at[(outer + UP_ORDER[p]) % 4, (z + 8 - p // 4 - 1 + lo) % 4, :, core]
        return remote(part, part, up_s.at[p], up_r.at[p], above)

    def down(p):
        part = w6.at[(outer + DOWN_ORDER[p]) % 4, (z + p // 4 + lo) % 4, :, core]
        return remote(part, part, dn_s.at[p], dn_r.at[p], below)

    def to_sibling(n):
        if n < 4:
            part = w6.at[(outer + n) % 4, z, :, core]
        elif n < 10:
            part = w6.at[(outer + UP_ORDER[n - 4]) % 4, (z + 3 - (n - 4) // 4) % 4, :, core]
        else:
            part = w6.at[(outer + DOWN_ORDER[n - 10]) % 4, (z + 1 + (n - 10) // 4) % 4, :, core]
        return remote(part, part, sib_s.at[n], sib_r.at[n], sibling)

    def first(axis, s, way, half):
        rows = pl.ds(half * (TOK // 2), TOK // 2)
        dst = cslot.at[axis, s, mine[axis], rows]
        src = dst if s else cot_hbm.at[rows, pl.ds(axis * 2 * SUB, SUB)]
        sems = axis, s, way, half
        return remote(src, dst, c1_s.at[sems], c1_r.at[sems], along[axis](1 + 2 * way))

    def second(axis, s, way):
        part = cslot.at[axis, s, (mine[axis] + 3 + 2 * way) % 4, pl.ds(way * (TOK // 2), TOK // 2)]
        return remote(part, part, c2_s.at[axis, s, way], c2_r.at[axis, s, way], along[axis](1 + 2 * way))

    def gated_to(axis, d):
        src = gsend.at[axis, (mine[axis] + d) % 4]
        dst = gt.at[axis, :, pl.ds(pl.multiple_of(mine[axis] * TOK, 128), TOK)]
        return remote(src, dst, gt_s.at[axis, d - 1], gt_r.at[axis, d - 1], along[axis](d))

    def own_gated(axis):
        src = gsend.at[axis, mine[axis]]
        dst = gt.at[axis, :, pl.ds(pl.multiple_of(mine[axis] * TOK, 128), TOK)]
        return pltpu.make_async_copy(src, dst, own_sem.at[axis])

    def stage2(n, d):
        return remote(
            p2s.at[n, d - 1], p2r.at[n, d - 1], s2_s.at[n, d - 1], s2_r.at[n, d - 1], along[1 - PIECES[n][0]](d)
        )

    def stage3(n, d):
        return remote(p3s.at[n, d - 1], p3r.at[n, d - 1], s3_s.at[n, d - 1], s3_r.at[n, d - 1], at_z(d))

    def exchange(n, way):
        device = (diagonal, across, sibling)[way]
        return remote(dec.at[n], dec_r.at[n, way], d_s.at[n, way], d_r.at[n, way], device)

    loads = [
        pltpu.make_async_copy(head_hbm, heads, load_sem.at[0]),
        pltpu.make_async_copy(gate_hbm, gates, load_sem.at[1]),
        pltpu.make_async_copy(
            w_hbm.at[pl.ds(pl.multiple_of(core * 16, 16), 16)], w6.at[outer, z, inner, core], load_sem.at[2]
        ),
    ]
    for axis in range(2):
        for s in range(2):
            loads.append(
                pltpu.make_async_copy(
                    cot_hbm.at[:, pl.ds((axis * 2 + s) * SUB, SUB)],
                    cslot.at[axis, s, mine[axis]],
                    load_sem.at[3 + axis * 2 + s],
                )
            )
    loads += [
        pltpu.make_async_copy(cot_hbm, cot, load_sem.at[7]),
        pltpu.make_async_copy(mom_hbm, mom, load_sem.at[8]),
        pltpu.make_async_copy(idx_hbm, idx, load_sem.at[9]),
    ]
    for load in loads:
        load.start()

    barrier = pltpu.get_barrier_semaphore()
    partners = [at(d) for at in (at_x, at_y, at_z) for d in (1, 2, 3)] + [sibling, diagonal, above, below]
    for device in partners:
        pl.semaphore_signal(barrier, inc=1, device_id=device, device_id_type=MESH)
    pl.semaphore_wait(barrier, len(partners))

    for d in (1, 2, 3):
        w1(d).start()
    for way in range(2):
        first(0, 0, way, way).start()
        first(1, 0, way, way).start()

    gain = gain_ref[...]
    loads[0].wait()
    loads[1].wait()

    def gated_block(b, carry):
        for k in range(4):
            cols = pl.ds(pl.multiple_of(b * SUB + k * HDIM, HDIM), HDIM)
            h = heads[:, cols].astype(F32)
            a = gates[:, cols].astype(F32)
            n = h * lax.rsqrt(jnp.mean(h * h, axis=-1, keepdims=True) + EPS)
            low = ((n * gain) * (a * jax.nn.sigmoid(a))).astype(BF16)
            turned = low.T
            gsend[1, b, k * 128 : (k + 1) * 128, :] = turned
            for to in range(4):
                rows = pl.ds(pl.multiple_of(b * 128 + k * 32, 32), 32)
                gsend[0, to, rows, :] = turned[to * 32 : (to + 1) * 32]
        return carry

    lax.fori_loop(0, 1, gated_block, 0)

    for load in loads[2:]:
        load.wait()
    for d in (1, 2, 3):
        w1(d).wait_recv()
    for d in (1, 3, 2):
        w2(d).start()
    @pl.when(lo == 1)
    def _():
        up(0).start()

    @pl.when(lo == 0)
    def _():
        down(0).start()

    to_sibling(0).start()

    lax.fori_loop(1, 4, gated_block, 0)
    for axis in range(2):
        own_gated(axis).start()

    def relay(p):
        @pl.when(lo == 0)
        def _():
            up(p).wait_recv()
            up(p).start()
            to_sibling(4 + p).start()

        @pl.when(lo == 1)
        def _():
            down(p).wait_recv()
            down(p).start()
            to_sibling(10 + p).start()

    def follow(p):
        @pl.when(lo == 0)
        def _():
            down(p).wait_recv()
            if p in (1, 3):
                down(p // 2 + 4).start()
            to_sibling(10 + p).start()

        @pl.when(lo == 1)
        def _():
            up(p).wait_recv()
            if p < 2:
                up(p + 4).start()
            to_sibling(4 + p).start()

    def terms(n):
        axis, s = PIECES[n]
        owners = [(mine[1 - axis] + d) % 4 for d in (1, 2, 3, 0)]
        if axis == 0:
            starts = [owner * 128 for owner in owners]
            left = [gt[0, pl.ds(pl.multiple_of(v, 128), 128), :] for v in starts]
        else:
            starts = [k * 128 + owner * 32 for owner in owners for k in range(4)]
            left = [gt[1, pl.ds(pl.multiple_of(v, 32), 32), :] for v in starts]
        part = jnp.dot(
            jnp.concatenate(left, axis=0), cslot[axis, s].reshape(4 * TOK, SUB), preferred_element_type=F32
        )
        for d in (2, 1, 3):
            p2s[n, d - 1] = part[(d - 1) * 128 : d * 128].astype(BF16)
            stage2(n, d).start()
        q[n] = part[384:]

    def pass_second(axis, s):
        for way in range(2):
            first(axis, s, way, way).wait_recv()
            second(axis, s, way).start()

    def own_piece(j):
        @pl.when(lo == 1)
        def _():
            up(UP_ORDER.index(j)).start()

        @pl.when(lo == 0)
        def _():
            down(DOWN_ORDER.index(j)).start()

        to_sibling(j).start()

    def second_in(axis, s):
        for way in range(2):
            first(axis, s, way, 1 - way).wait_recv()
            second(axis, s, way).wait_recv()

    def sum2(n):
        for d in (1, 2, 3):
            stage2(n, d).wait_recv()
        q[n] += (p2r[n, 0].astype(F32) + p2r[n, 1].astype(F32)) + p2r[n, 2].astype(F32)
        for d in (2, 1, 3):
            rows = pl.ds(pl.multiple_of(((z + d) % 4) * ROWS, ROWS), ROWS)
            p3s[n, d - 1] = q[n, rows, :].astype(BF16)
            stage3(n, d).start()

    def gated_in(axis):
        own_gated(axis).wait()
        for d in (1, 2, 3):
            gated_to(axis, d).wait_recv()

    def stacked(v):
        return jnp.concatenate([v[:, k * 128 : (k + 1) * 128] for k in range(4)], axis=0)

    def choose():
        row = lax.broadcasted_iota(jnp.int32, (SUB, SUB), 0)
        col = lax.broadcasted_iota(jnp.int32, (SUB, SUB), 1)
        same = (((row >> 4) & 7) == (col >> 6)) & ((row >> 7) == ((col >> 4) & 3))
        spread = jnp.where(same, 1.0, 0.0).astype(BF16)
        where = stacked(idx[...])
        bits = jnp.left_shift(jnp.ones_like(where), where & 15)
        bits = jnp.concatenate(
            [jnp.where((where >> 4) == k, bits, 0).astype(F32).astype(BF16) for k in range(4)], axis=1
        )
        words = jnp.dot(bits, spread, preferred_element_type=F32).astype(jnp.int32)
        lane = lax.broadcasted_iota(jnp.int32, (4 * ROWS, SUB), 1)
        kept = (lax.shift_right_logical(words, lane & 15) & 1).astype(F32)
        for n in range(4):
            axis, s = PIECES[n]
            piece = axis * 2 + s
            chosen[n] = stacked(kept[piece * ROWS : (piece + 1) * ROWS])

    def moment_step(n):
        axis, s = PIECES[n]
        start = (axis * 2 + s) * SUB
        for d in (1, 2, 3):
            stage3(n, d).wait_recv()
        own = q[n, pl.ds(pl.multiple_of(z * ROWS, ROWS), ROWS), :]
        gradient = (own + p3r[n, 0].astype(F32)) + (p3r[n, 1].astype(F32) + p3r[n, 2].astype(F32))
        moment = DECAY * mom[:, start : start + SUB] + gradient * ((TOK * 64) ** -0.5)
        coeffs = jnp.dot(stacked(moment), dct_ref[...], precision=HIGHEST, preferred_element_type=F32)
        decoded = jnp.dot(
            coeffs * chosen[n], idct_ref[...], precision=HIGHEST, preferred_element_type=F32
        )
        decoded = jnp.concatenate([decoded[k * ROWS : (k + 1) * ROWS] for k in range(4)], axis=1)
        dec[n] = decoded
        for way in range(3):
            exchange(n, way).start()
        newmom[:, start : start + SUB] = moment - decoded

    def update_step(n):
        axis, s = PIECES[n]
        start = (axis * 2 + s) * SUB
        for way in range(3):
            exchange(n, way).wait_recv()
        update[:, start : start + SUB] = ((dec[n] + dec_r[n, 2]) + (dec_r[n, 0] + dec_r[n, 1])) * 0.25

    def back(block, ys):
        halves = []
        for v in ys:
            for k in range(4):
                halves += [w6[v, block, k, 0], w6[k, block, v, 1]]
        weight = jnp.concatenate(halves, axis=0)
        both = lax.dot_general(cot[...], weight, (((1,), (1,)), ((), ())), preferred_element_type=F32)
        for part in range(len(ys)):
            head = ys[part] * 4 + block
            cols = pl.ds(pl.multiple_of(head * HDIM, HDIM), HDIM)
            u = both[:, part * HDIM : (part + 1) * HDIM]
            h = heads[:, cols].astype(F32)
            a = gates[:, cols].astype(F32)
            r = lax.rsqrt(jnp.mean(h * h, axis=-1, keepdims=True) + EPS)
            n = h * r
            sig = jax.nn.sigmoid(a)
            ggrad[:, cols] = ((u * (n * gain)) * (sig * (1.0 + a * (1.0 - sig)))).astype(BF16)
            ds = (u * (a * sig)) * gain
            hgrad[:, cols] = (r * (ds - n * jnp.mean(ds * n, axis=-1, keepdims=True))).astype(BF16)

    prev, prev2, after = (z + 3) % 4, (z + 2) % 4, (z + 1) % 4

    def block_back(block, arrivals):
        for n in arrivals:
            to_sibling(n).wait_recv()
        back(block, (0, 1))
        back(block, (2, 3))

    for way in range(2):
        first(0, 0, way, 1 - way).start()
        first(1, 0, way, 1 - way).start()
    for d in (1, 3, 2):
        for axis in range(2):
            gated_to(axis, d).start()
    choose()
    for j in (1, 3):
        w2(4 - j).wait_recv()
        own_piece(j)
    w2(2).wait_recv()
    own_piece(2)
    pass_second(0, 0)
    pass_second(1, 0)
    for half in range(2):
        for way in range(2):
            first(0, 1, way, (way + half) % 2).start()
            first(1, 1, way, (way + half) % 2).start()
    relay(0)
    follow(0)
    relay(1)
    block_back(z, range(4))
    relay(2)
    follow(1)
    relay(3)
    follow(2)
    relay(4)
    follow(3)
    gated_in(0)
    second_in(0, 0)
    terms(0)
    gated_in(1)
    second_in(1, 0)
    terms(1)
    pass_second(0, 1)
    pass_second(1, 1)
    relay(5)
    follow(4)
    block_back(prev, range(4, 8))
    block_back(after, range(10, 14))
    follow(5)
    sum2(0)
    sum2(1)
    second_in(0, 1)
    terms(2)
    second_in(1, 1)
    terms(3)
    moment_step(0)
    moment_step(1)
    block_back(prev2, (8, 9, 14, 15))
    sum2(2)
    sum2(3)
    update_step(0)
    update_step(1)
    moment_step(2)
    moment_step(3)
    update_step(2)
    update_step(3)

    for d in (1, 2, 3):
        w1(d).wait_send()
        w2(d).wait_send()
        for axis in range(2):
            gated_to(axis, d).wait_send()
        for n in range(4):
            stage2(n, d).wait_send()
            stage3(n, d).wait_send()
    for p in range(6):
        up(p).wait_send()
        down(p).wait_send()
    for n in range(16):
        to_sibling(n).wait_send()
    for axis in range(2):
        for s in range(2):
            for way in range(2):
                first(axis, s, way, 0).wait_send()
                first(axis, s, way, 1).wait_send()
                second(axis, s, way).wait_send()
    for n in range(4):
        for way in range(3):
            exchange(n, way).wait_send()


def place(*refs):
    sources, targets, sem = refs[:4], refs[4:8], refs[8]
    copies = []
    for n in range(4):
        rows = sources[n].shape[0] // 2
        for half in range(2):
            part = pl.ds(half * rows, rows)
            copies.append(
                pltpu.make_async_copy(sources[n].at[part], targets[n].at[part], sem.at[n * 2 + half])
            )
    for copy in copies:
        copy.start()
    for copy in copies:
        copy.wait()


def cosine_pair():
    freq = np.arange(SPAN)[:, None]
    place = np.arange(SPAN)[None, :]
    table = np.cos(np.pi * (place + 0.5) * freq / SPAN) * np.where(
        freq == 0, np.sqrt(1.0 / SPAN), np.sqrt(2.0 / SPAN)
    )
    inverse = np.kron(np.eye(2), table)
    return np.ascontiguousarray(inverse.T).astype(np.float32), inverse.astype(np.float32)


def local(head_out, gate_in, cotangent, momentum, chosen_index, out_weight, norm_gain):
    forward, inverse = cosine_pair()
    anywhere = pl.BlockSpec(memory_space=pl.ANY)
    vmem = pl.BlockSpec(memory_space=pltpu.VMEM)
    dma = pltpu.SemaphoreType.DMA
    scratch = [
        pltpu.VMEM((TOK, WIDTH), BF16),
        pltpu.VMEM((TOK, WIDTH), BF16),
        pltpu.VMEM((TOK, WIDTH), BF16),
        pltpu.VMEM((ROWS, WIDTH), F32),
        pltpu.VMEM((ROWS, WIDTH // 4), jnp.int32),
        pltpu.VMEM((4, 4, 4, 2, 16, WIDTH), BF16),
        pltpu.VMEM((2, 4, SUB, TOK), BF16),
        pltpu.VMEM((2, SUB, 4 * TOK), BF16),
        pltpu.VMEM((2, 2, 4, TOK, SUB), BF16),
        pltpu.VMEM((4, 3, 128, SUB), BF16),
        pltpu.VMEM((4, 3, 128, SUB), BF16),
        pltpu.VMEM((4, 128, SUB), F32),
        pltpu.VMEM((4, 3, ROWS, SUB), BF16),
        pltpu.VMEM((4, 3, ROWS, SUB), BF16),
        pltpu.VMEM((4, ROWS, SUB), F32),
        pltpu.VMEM((4, 3, ROWS, SUB), F32),
        pltpu.VMEM((4, 128, 128), F32),
        dma((10,)), dma((2,)),
        dma((3,)), dma((3,)), dma((3,)), dma((3,)),
        dma((6,)), dma((6,)), dma((6,)), dma((6,)),
        dma((16,)), dma((16,)),
        dma((2, 2, 2, 2)), dma((2, 2, 2, 2)), dma((2, 2, 2)), dma((2, 2, 2)),
        dma((2, 3)), dma((2, 3)),
        dma((4, 3)), dma((4, 3)), dma((4, 3)), dma((4, 3)),
        dma((4, 3)), dma((4, 3)),
    ]
    results = pl.pallas_call(
        kernel,
        name="demo_step",
        out_shape=(
            pltpu.VMEM((TOK, WIDTH), BF16),
            pltpu.VMEM((TOK, WIDTH), BF16),
            pltpu.VMEM((ROWS, WIDTH), F32),
            pltpu.VMEM((ROWS, WIDTH), F32),
        ),
        in_specs=[anywhere] * 6 + [vmem] * 3,
        out_specs=(vmem,) * 4,
        scratch_shapes=scratch,
        compiler_params=pltpu.CompilerParams(
            collective_id=0, has_side_effects=True, vmem_limit_bytes=60 * 2**20 + 2**18
        ),
        cost_estimate=pl.CostEstimate(flops=14 * 10**9, bytes_accessed=9 * 10**6, transcendentals=10**6),
    )(
        head_out[0], gate_in[0], cotangent[0], momentum[0], chosen_index[0], out_weight,
        norm_gain.reshape(1, HDIM), jnp.asarray(forward), jnp.asarray(inverse),
    )
    head_grad, gate_grad, new_momentum, update = pl.pallas_call(
        place,
        name="place_results",
        out_shape=tuple(jax.ShapeDtypeStruct(v.shape, v.dtype) for v in results),
        in_specs=[vmem] * 4,
        out_specs=(anywhere,) * 4,
        scratch_shapes=[dma((8,))],
        compiler_params=pltpu.CompilerParams(vmem_limit_bytes=2**20),
    )(*(pltpu.with_memory_space_constraint(v, pltpu.VMEM) for v in results))
    return head_grad[None], gate_grad[None], new_momentum[None], update


def solution(mesh):
    rows = P("group", "fsdp", None)
    return jax.shard_map(
        local,
        mesh=mesh,
        in_specs=(rows, rows, rows, rows, rows, P("fsdp", None), P()),
        out_specs=(rows, rows, rows, P("fsdp", None)),
        check_vma=False,
    )
```

```python
import functools

import jax
import jax.numpy as jnp
import numpy as np
from jax import lax
from jax.experimental import pallas as pl
from jax.experimental.pallas import tpu as pltpu
from jax.sharding import PartitionSpec as P

MESH = pl.DeviceIdType.MESH
HIGHEST = lax.Precision.HIGHEST
F32 = jnp.float32
BF16 = jnp.bfloat16

SPAN = 64
KEEP = 16
HDIM = 128
TOK = 384
WIDTH = 2048
ROWS = 32
SUB = 512
EPS = 1e-06
DECAY = 0.999

PIECES = ((0, 0), (1, 0), (0, 1), (1, 1))

UP_ORDER = (0, 1, 3, 2, 0, 1)
DOWN_ORDER = (0, 3, 1, 2, 3, 2)


def remote(src, dst, send, recv, device):
    return pltpu.make_async_remote_copy(
        src_ref=src, dst_ref=dst, send_sem=send, recv_sem=recv, device_id=device, device_id_type=MESH
    )


def kernel(
    head_hbm, gate_hbm, cot_hbm, mom_hbm, idx_hbm, w_hbm, gain_hbm, dct_hbm, idct_hbm,
    hgrad, ggrad, newmom, update,
    heads, gates, cot, mom, idx, w6, gsend, gt, cslot, p2s, p2r, q, p3s, p3r, dec, dec_r, chosen, gain_ref, dct_ref, idct_ref,
    load_sem, own_sem,
    w1_s, w1_r, w2_s, w2_r, up_s, up_r, dn_s, dn_r, sib_s, sib_r,
    c1_s, c1_r, c2_s, c2_r, gt_s, gt_r, s2_s, s2_r, s3_s, s3_r, d_s, d_r,
):
    f = lax.axis_index("fsdp")
    g = lax.axis_index("group")
    y, z, x = f // 16, (f // 4) % 4, f % 4
    lo, core = g // 2, g % 2
    sibling = {"fsdp": f, "group": g + 1 - 2 * core}
    across = {"fsdp": f, "group": (g + 2) % 4}
    diagonal = {"fsdp": f, "group": 3 - g}
    above = {"fsdp": y * 16 + ((z + lo) % 4) * 4 + x, "group": (g + 2) % 4}
    below = {"fsdp": y * 16 + ((z + 3 + lo) % 4) * 4 + x, "group": (g + 2) % 4}

    def at_x(d):
        return {"fsdp": y * 16 + z * 4 + (x + d) % 4, "group": g}

    def at_y(d):
        return {"fsdp": ((y + d) % 4) * 16 + z * 4 + x, "group": g}

    def at_z(d):
        return {"fsdp": y * 16 + ((z + d) % 4) * 4 + x, "group": g}

    along = (at_x, at_y)
    mine = (x, y)

    outer = (1 - core) * y + core * x
    inner = (1 - core) * x + core * y

    def at_inner(d):
        return {"fsdp": (1 - core) * at_x(d)["fsdp"] + core * at_y(d)["fsdp"], "group": g}

    def at_outer(d):
        return {"fsdp": (1 - core) * at_y(d)["fsdp"] + core * at_x(d)["fsdp"], "group": g}

    def w1(d):
        half = w_hbm.at[pl.ds(pl.multiple_of(core * 16, 16), 16)]
        return remote(half, w6.at[outer, z, inner, core], w1_s.at[d - 1], w1_r.at[d - 1], at_inner(d))

    def w2(d):
        part = w6.at[outer, z, :, core]
        return remote(part, part, w2_s.at[d - 1], w2_r.at[d - 1], at_outer(d))

    def up(p):
        part = w6.at[(outer + UP_ORDER[p]) % 4, (z + 8 - p // 4 - 1 + lo) % 4, :, core]
        return remote(part, part, up_s.at[p], up_r.at[p], above)

    def down(p):
        part = w6.at[(outer + DOWN_ORDER[p]) % 4, (z + p // 4 + lo) % 4, :, core]
        return remote(part, part, dn_s.at[p], dn_r.at[p], below)

    def to_sibling(n):
        if n < 4:
            part = w6.at[(outer + n) % 4, z, :, core]
        elif n < 10:
            part = w6.at[(outer + UP_ORDER[n - 4]) % 4, (z + 3 - (n - 4) // 4) % 4, :, core]
        else:
            part = w6.at[(outer + DOWN_ORDER[n - 10]) % 4, (z + 1 + (n - 10) // 4) % 4, :, core]
        return remote(part, part, sib_s.at[n], sib_r.at[n], sibling)

    def first(axis, s, way, half):
        rows = pl.ds(half * (TOK // 2), TOK // 2)
        dst = cslot.at[axis, s, mine[axis], rows]
        src = dst if s else cot_hbm.at[rows, pl.ds(axis * 2 * SUB, SUB)]
        sems = axis, s, way, half
        return remote(src, dst, c1_s.at[sems], c1_r.at[sems], along[axis](1 + 2 * way))

    def second(axis, s, way):
        part = cslot.at[axis, s, (mine[axis] + 3 + 2 * way) % 4, pl.ds(way * (TOK // 2), TOK // 2)]
        return remote(part, part, c2_s.at[axis, s, way], c2_r.at[axis, s, way], along[axis](1 + 2 * way))

    def gated_to(axis, d):
        src = gsend.at[axis, (mine[axis] + d) % 4]
        dst = gt.at[axis, :, pl.ds(pl.multiple_of(mine[axis] * TOK, 128), TOK)]
        return remote(src, dst, gt_s.at[axis, d - 1], gt_r.at[axis, d - 1], along[axis](d))

    def own_gated(axis):
        src = gsend.at[axis, mine[axis]]
        dst = gt.at[axis, :, pl.ds(pl.multiple_of(mine[axis] * TOK, 128), TOK)]
        return pltpu.make_async_copy(src, dst, own_sem.at[axis])

    def stage2(n, d):
        return remote(
            p2s.at[n, d - 1], p2r.at[n, d - 1], s2_s.at[n, d - 1], s2_r.at[n, d - 1], along[1 - PIECES[n][0]](d)
        )

    def stage3(n, d):
        return remote(p3s.at[n, d - 1], p3r.at[n, d - 1], s3_s.at[n, d - 1], s3_r.at[n, d - 1], at_z(d))

    def exchange(n, way):
        device = (diagonal, across, sibling)[way]
        return remote(dec.at[n], dec_r.at[n, way], d_s.at[n, way], d_r.at[n, way], device)

    loads = [
        pltpu.make_async_copy(head_hbm, heads, load_sem.at[0]),
        pltpu.make_async_copy(gate_hbm, gates, load_sem.at[1]),
        pltpu.make_async_copy(
            w_hbm.at[pl.ds(pl.multiple_of(core * 16, 16), 16)], w6.at[outer, z, inner, core], load_sem.at[2]
        ),
    ]
    for axis in range(2):
        for s in range(2):
            loads.append(
                pltpu.make_async_copy(
                    cot_hbm.at[:, pl.ds((axis * 2 + s) * SUB, SUB)],
                    cslot.at[axis, s, mine[axis]],
                    load_sem.at[3 + axis * 2 + s],
                )
            )
    loads += [
        pltpu.make_async_copy(cot_hbm, cot, load_sem.at[7]),
        pltpu.make_async_copy(mom_hbm, mom, load_sem.at[8]),
        pltpu.make_async_copy(idx_hbm, idx, load_sem.at[9]),
        pltpu.make_async_copy(dct_hbm, dct_ref, load_sem.at[10]),
        pltpu.make_async_copy(idct_hbm, idct_ref, load_sem.at[11]),
    ]
    gain_load = pltpu.make_async_copy(gain_hbm, gain_ref, load_sem.at[12])
    gain_load.start()
    for load in loads:
        load.start()

    barrier = pltpu.get_barrier_semaphore()
    partners = [at(d) for at in (at_x, at_y, at_z) for d in (1, 2, 3)] + [sibling, diagonal, above, below]
    for device in partners:
        pl.semaphore_signal(barrier, inc=1, device_id=device, device_id_type=MESH)
    pl.semaphore_wait(barrier, len(partners))

    for d in (1, 2, 3):
        w1(d).start()
    for way in range(2):
        first(0, 0, way, way).start()
        first(1, 0, way, way).start()

    gain_load.wait()
    gain = gain_ref[...]
    loads[0].wait()
    loads[1].wait()

    def gated_block(b, carry):
        for k in range(4):
            cols = pl.ds(pl.multiple_of(b * SUB + k * HDIM, HDIM), HDIM)
            h = heads[:, cols].astype(F32)
            a = gates[:, cols].astype(F32)
            n = h * lax.rsqrt(jnp.mean(h * h, axis=-1, keepdims=True) + EPS)
            low = ((n * gain) * (a * jax.nn.sigmoid(a))).astype(BF16)
            turned = low.T
            gsend[1, b, k * 128 : (k + 1) * 128, :] = turned
            for to in range(4):
                rows = pl.ds(pl.multiple_of(b * 128 + k * 32, 32), 32)
                gsend[0, to, rows, :] = turned[to * 32 : (to + 1) * 32]
        return carry

    lax.fori_loop(0, 1, gated_block, 0)

    for load in loads[2:]:
        load.wait()
    for d in (1, 2, 3):
        w1(d).wait_recv()
    for d in (1, 3, 2):
        w2(d).start()
    @pl.when(lo == 1)
    def _():
        up(0).start()

    @pl.when(lo == 0)
    def _():
        down(0).start()

    to_sibling(0).start()

    lax.fori_loop(1, 4, gated_block, 0)
    for axis in range(2):
        own_gated(axis).start()

    def relay(p):
        @pl.when(lo == 0)
        def _():
            up(p).wait_recv()
            up(p).start()
            to_sibling(4 + p).start()

        @pl.when(lo == 1)
        def _():
            down(p).wait_recv()
            down(p).start()
            to_sibling(10 + p).start()

    def follow(p):
        @pl.when(lo == 0)
        def _():
            down(p).wait_recv()
            if p in (1, 3):
                down(p // 2 + 4).start()
            to_sibling(10 + p).start()

        @pl.when(lo == 1)
        def _():
            up(p).wait_recv()
            if p < 2:
                up(p + 4).start()
            to_sibling(4 + p).start()

    def terms(n):
        axis, s = PIECES[n]
        owners = [(mine[1 - axis] + d) % 4 for d in (1, 2, 3, 0)]
        if axis == 0:
            starts = [owner * 128 for owner in owners]
            left = [gt[0, pl.ds(pl.multiple_of(v, 128), 128), :] for v in starts]
        else:
            starts = [k * 128 + owner * 32 for owner in owners for k in range(4)]
            left = [gt[1, pl.ds(pl.multiple_of(v, 32), 32), :] for v in starts]
        part = jnp.dot(
            jnp.concatenate(left, axis=0), cslot[axis, s].reshape(4 * TOK, SUB), preferred_element_type=F32
        )
        for d in (2, 1, 3):
            p2s[n, d - 1] = part[(d - 1) * 128 : d * 128].astype(BF16)
            stage2(n, d).start()
        q[n] = part[384:]

    def pass_second(axis, s):
        for way in range(2):
            first(axis, s, way, way).wait_recv()
            second(axis, s, way).start()

    def own_piece(j):
        @pl.when(lo == 1)
        def _():
            up(UP_ORDER.index(j)).start()

        @pl.when(lo == 0)
        def _():
            down(DOWN_ORDER.index(j)).start()

        to_sibling(j).start()

    def second_in(axis, s):
        for way in range(2):
            first(axis, s, way, 1 - way).wait_recv()
            second(axis, s, way).wait_recv()

    def sum2(n):
        for d in (1, 2, 3):
            stage2(n, d).wait_recv()
        q[n] += (p2r[n, 0].astype(F32) + p2r[n, 1].astype(F32)) + p2r[n, 2].astype(F32)
        for d in (2, 1, 3):
            rows = pl.ds(pl.multiple_of(((z + d) % 4) * ROWS, ROWS), ROWS)
            p3s[n, d - 1] = q[n, rows, :].astype(BF16)
            stage3(n, d).start()

    def gated_in(axis):
        own_gated(axis).wait()
        for d in (1, 2, 3):
            gated_to(axis, d).wait_recv()

    def stacked(v):
        return jnp.concatenate([v[:, k * 128 : (k + 1) * 128] for k in range(4)], axis=0)

    def choose():
        row = lax.broadcasted_iota(jnp.int32, (SUB, SUB), 0)
        col = lax.broadcasted_iota(jnp.int32, (SUB, SUB), 1)
        same = (((row >> 4) & 7) == (col >> 6)) & ((row >> 7) == ((col >> 4) & 3))
        spread = jnp.where(same, 1.0, 0.0).astype(BF16)
        where = stacked(idx[...])
        bits = jnp.left_shift(jnp.ones_like(where), where & 15)
        bits = jnp.concatenate(
            [jnp.where((where >> 4) == k, bits, 0).astype(F32).astype(BF16) for k in range(4)], axis=1
        )
        words = jnp.dot(bits, spread, preferred_element_type=F32).astype(jnp.int32)
        lane = lax.broadcasted_iota(jnp.int32, (4 * ROWS, SUB), 1)
        kept = (lax.shift_right_logical(words, lane & 15) & 1).astype(F32)
        for n in range(4):
            axis, s = PIECES[n]
            piece = axis * 2 + s
            chosen[n] = stacked(kept[piece * ROWS : (piece + 1) * ROWS])

    def moment_step(n):
        axis, s = PIECES[n]
        start = (axis * 2 + s) * SUB
        for d in (1, 2, 3):
            stage3(n, d).wait_recv()
        own = q[n, pl.ds(pl.multiple_of(z * ROWS, ROWS), ROWS), :]
        gradient = (own + p3r[n, 0].astype(F32)) + (p3r[n, 1].astype(F32) + p3r[n, 2].astype(F32))
        moment = DECAY * mom[:, start : start + SUB] + gradient * ((TOK * 64) ** -0.5)
        coeffs = jnp.dot(stacked(moment), dct_ref[...], precision=HIGHEST, preferred_element_type=F32)
        decoded = jnp.dot(
            coeffs * chosen[n], idct_ref[...], precision=HIGHEST, preferred_element_type=F32
        )
        decoded = jnp.concatenate([decoded[k * ROWS : (k + 1) * ROWS] for k in range(4)], axis=1)
        dec[n] = decoded
        for way in range(3):
            exchange(n, way).start()
        newmom[:, start : start + SUB] = moment - decoded

    def update_step(n):
        axis, s = PIECES[n]
        start = (axis * 2 + s) * SUB
        for way in range(3):
            exchange(n, way).wait_recv()
        update[:, start : start + SUB] = ((dec[n] + dec_r[n, 2]) + (dec_r[n, 0] + dec_r[n, 1])) * 0.25

    def back(block, ys):
        halves = []
        for v in ys:
            for k in range(4):
                halves += [w6[v, block, k, 0], w6[k, block, v, 1]]
        weight = jnp.concatenate(halves, axis=0)
        both = lax.dot_general(cot[...], weight, (((1,), (1,)), ((), ())), preferred_element_type=F32)
        for part in range(len(ys)):
            head = ys[part] * 4 + block
            cols = pl.ds(pl.multiple_of(head * HDIM, HDIM), HDIM)
            u = both[:, part * HDIM : (part + 1) * HDIM]
            h = heads[:, cols].astype(F32)
            a = gates[:, cols].astype(F32)
            r = lax.rsqrt(jnp.mean(h * h, axis=-1, keepdims=True) + EPS)
            n = h * r
            sig = jax.nn.sigmoid(a)
            ggrad[:, cols] = ((u * (n * gain)) * (sig * (1.0 + a * (1.0 - sig)))).astype(BF16)
            ds = (u * (a * sig)) * gain
            hgrad[:, cols] = (r * (ds - n * jnp.mean(ds * n, axis=-1, keepdims=True))).astype(BF16)

    prev, prev2, after = (z + 3) % 4, (z + 2) % 4, (z + 1) % 4

    def block_back(block, arrivals):
        for n in arrivals:
            to_sibling(n).wait_recv()
        back(block, (0, 1))
        back(block, (2, 3))

    for way in range(2):
        first(0, 0, way, 1 - way).start()
        first(1, 0, way, 1 - way).start()
    for d in (1, 3, 2):
        for axis in range(2):
            gated_to(axis, d).start()
    choose()
    for j in (1, 3):
        w2(4 - j).wait_recv()
        own_piece(j)
    w2(2).wait_recv()
    own_piece(2)
    pass_second(0, 0)
    pass_second(1, 0)
    for half in range(2):
        for way in range(2):
            first(0, 1, way, (way + half) % 2).start()
            first(1, 1, way, (way + half) % 2).start()
    relay(0)
    follow(0)
    relay(1)
    block_back(z, range(4))
    relay(2)
    follow(1)
    relay(3)
    follow(2)
    relay(4)
    follow(3)
    gated_in(0)
    second_in(0, 0)
    terms(0)
    gated_in(1)
    second_in(1, 0)
    terms(1)
    pass_second(0, 1)
    pass_second(1, 1)
    relay(5)
    follow(4)
    block_back(prev, range(4, 8))
    block_back(after, range(10, 14))
    follow(5)
    sum2(0)
    sum2(1)
    second_in(0, 1)
    terms(2)
    second_in(1, 1)
    terms(3)
    moment_step(0)
    moment_step(1)
    block_back(prev2, (8, 9, 14, 15))
    sum2(2)
    sum2(3)
    update_step(0)
    update_step(1)
    moment_step(2)
    moment_step(3)
    update_step(2)
    update_step(3)

    for d in (1, 2, 3):
        w1(d).wait_send()
        w2(d).wait_send()
        for axis in range(2):
            gated_to(axis, d).wait_send()
        for n in range(4):
            stage2(n, d).wait_send()
            stage3(n, d).wait_send()
    for p in range(6):
        up(p).wait_send()
        down(p).wait_send()
    for n in range(16):
        to_sibling(n).wait_send()
    for axis in range(2):
        for s in range(2):
            for way in range(2):
                first(axis, s, way, 0).wait_send()
                first(axis, s, way, 1).wait_send()
                second(axis, s, way).wait_send()
    for n in range(4):
        for way in range(3):
            exchange(n, way).wait_send()


def place(*refs):
    sources, targets, sem = refs[:4], refs[4:8], refs[8]
    copies = []
    for n in range(4):
        rows = sources[n].shape[0] // 2
        for half in range(2):
            part = pl.ds(half * rows, rows)
            copies.append(
                pltpu.make_async_copy(sources[n].at[part], targets[n].at[part], sem.at[n * 2 + half])
            )
    for copy in copies:
        copy.start()
    for copy in copies:
        copy.wait()


def cosine_pair():
    freq = np.arange(SPAN)[:, None]
    place = np.arange(SPAN)[None, :]
    table = np.cos(np.pi * (place + 0.5) * freq / SPAN) * np.where(
        freq == 0, np.sqrt(1.0 / SPAN), np.sqrt(2.0 / SPAN)
    )
    inverse = np.kron(np.eye(2), table)
    return np.ascontiguousarray(inverse.T).astype(np.float32), inverse.astype(np.float32)


def local(head_out, gate_in, cotangent, momentum, chosen_index, out_weight, norm_gain):
    forward, inverse = cosine_pair()
    anywhere = pl.BlockSpec(memory_space=pl.ANY)
    vmem = pl.BlockSpec(memory_space=pltpu.VMEM)
    dma = pltpu.SemaphoreType.DMA
    scratch = [
        pltpu.VMEM((TOK, WIDTH), BF16),
        pltpu.VMEM((TOK, WIDTH), BF16),
        pltpu.VMEM((TOK, WIDTH), BF16),
        pltpu.VMEM((ROWS, WIDTH), F32),
        pltpu.VMEM((ROWS, WIDTH // 4), jnp.int32),
        pltpu.VMEM((4, 4, 4, 2, 16, WIDTH), BF16),
        pltpu.VMEM((2, 4, SUB, TOK), BF16),
        pltpu.VMEM((2, SUB, 4 * TOK), BF16),
        pltpu.VMEM((2, 2, 4, TOK, SUB), BF16),
        pltpu.VMEM((4, 3, 128, SUB), BF16),
        pltpu.VMEM((4, 3, 128, SUB), BF16),
        pltpu.VMEM((4, 128, SUB), F32),
        pltpu.VMEM((4, 3, ROWS, SUB), BF16),
        pltpu.VMEM((4, 3, ROWS, SUB), BF16),
        pltpu.VMEM((4, ROWS, SUB), F32),
        pltpu.VMEM((4, 3, ROWS, SUB), F32),
        pltpu.VMEM((4, 128, 128), F32),
        pltpu.VMEM((1, HDIM), F32),
        pltpu.VMEM((128, 128), F32),
        pltpu.VMEM((128, 128), F32),
        dma((13,)), dma((2,)),
        dma((3,)), dma((3,)), dma((3,)), dma((3,)),
        dma((6,)), dma((6,)), dma((6,)), dma((6,)),
        dma((16,)), dma((16,)),
        dma((2, 2, 2, 2)), dma((2, 2, 2, 2)), dma((2, 2, 2)), dma((2, 2, 2)),
        dma((2, 3)), dma((2, 3)),
        dma((4, 3)), dma((4, 3)), dma((4, 3)), dma((4, 3)),
        dma((4, 3)), dma((4, 3)),
    ]
    results = pl.pallas_call(
        kernel,
        name="demo_step",
        out_shape=(
            pltpu.VMEM((TOK, WIDTH), BF16),
            pltpu.VMEM((TOK, WIDTH), BF16),
            pltpu.VMEM((ROWS, WIDTH), F32),
            pltpu.VMEM((ROWS, WIDTH), F32),
        ),
        in_specs=[anywhere] * 9,
        out_specs=(vmem,) * 4,
        scratch_shapes=scratch,
        compiler_params=pltpu.CompilerParams(
            collective_id=0, has_side_effects=True, vmem_limit_bytes=60 * 2**20 + 2**18
        ),
        cost_estimate=pl.CostEstimate(flops=14 * 10**9, bytes_accessed=9 * 10**6, transcendentals=10**6),
    )(
        head_out[0], gate_in[0], cotangent[0], momentum[0], chosen_index[0], out_weight,
        norm_gain.reshape(1, HDIM), jnp.asarray(forward), jnp.asarray(inverse),
    )
    head_grad, gate_grad, new_momentum, update = pl.pallas_call(
        place,
        name="place_results",
        out_shape=tuple(jax.ShapeDtypeStruct(v.shape, v.dtype) for v in results),
        in_specs=[vmem] * 4,
        out_specs=(anywhere,) * 4,
        scratch_shapes=[dma((8,))],
        compiler_params=pltpu.CompilerParams(vmem_limit_bytes=2**20),
    )(*(pltpu.with_memory_space_constraint(v, pltpu.VMEM) for v in results))
    return head_grad[None], gate_grad[None], new_momentum[None], update


def solution(mesh):
    rows = P("group", "fsdp", None)
    return jax.shard_map(
        local,
        mesh=mesh,
        in_specs=(rows, rows, rows, rows, rows, P("fsdp", None), P()),
        out_specs=(rows, rows, rows, P("fsdp", None)),
        check_vma=False,
    )
```
